32 devices in a mesh: groups: 2 (over y), dp: 8 (over z, x), tensor: 2 (over core).
Axes of the slice: x: 2, y: 2, z: 4, core: 2. Of those that a mesh axis runs over, the one named last changes fastest.
Arguments:
- activations: bfloat16 [4096, 13824], P(('groups', 'dp'), 'tensor'), parts along dimension 0, may hold values from -6 to 6
- out_grads: bfloat16 [4096, 5120], P(('groups', 'dp'), 'tensor'), parts along dimension 0, may hold values from -6 to 6
- act_factor: bfloat16 [640, 13824], P('dp', 'tensor'), may hold values from -0.009765625 to 0.009765625
- grad_factor: bfloat16 [640, 5120], P('dp', 'tensor'), may hold values from -0.015625 to 0.015625
- query_of_row: int32 [640], replicated, may hold values from 0 to 19, as said below
- live_tokens: int32 [128], P(('groups', 'dp')), parts along dimension 0, may hold values from 0 to 32, as said below
- move_plan: int32 [128, 2], P(('groups', 'dp')), parts along dimension 0, may hold values from -1 to 7, as said below
Outputs:
- influence: float32 [64, 20], P(('groups', 'dp')), parts along dimension 0
The draws below stay inside these ranges and needn't reach their ends.
There are 2 independent parts, one for each index of `groups`. The reference program is written for one: setup_inputs(seed, part) draws one part's arguments, and reference() takes and returns one part's arrays. A program takes and returns all parts, laid end to end along the dimension named above; an argument that names none is the same for every part. Nothing has to cross between parts.
Inputs may be any that keep to these rules, and one draw needn't show every extreme that they name: query_of_row names every query by exactly 32 rows. `live_tokens`: 0 where the slot's move_plan entry is -1, else 1 to 32; live tokens stand at the front of a block. `move_plan`: entry s is -1, -1 for an empty slot; else a live block of device d (slots d * 8 to (d + 1) * 8 - 1) goes to device d, d + 1 or d - 1 along the closed dp loop (indices modulo 8); blocks from device d - 1 land in slots below 2, blocks from device d + 1 in slots 2 and above; at most 2 blocks of one device go to each neighbour; each of the 32 destinations receives exactly one block; some device has all 8 slots live.
All inputs are finite; a program needn't handle non-finite values.
Results may differ from the reference program's by a relative error of at most 0.0003.
Values may be sent and summed in bfloat16 or wider, within the bound.
No kernel may reach another device: no remote copies, remote signals or barrier semaphores. Data moves between devices by JAX's collectives and lax.ppermute only.
A program may use at most 128 MiB of HBM per device.

```python
import jax
import jax.numpy as jnp
from jax import lax

D = 5120
HID = 13824
RANK = 32
QUERIES = 20
BLOCK = 32
SLOTS_OUT = 4
MOVE = 2
SLOTS_IN = 8
QR = 640
TOKENS_IN = 2048
N_DP = 8


def build_plan(key):
    key = jax.random.fold_in(key, 11)
    subkeys = jax.random.split(key, 6)
    go_right = jax.random.randint(subkeys[0], (N_DP,), 0, MOVE + 1)
    go_left = jax.random.randint(subkeys[1], (N_DP,), 0, MOVE + 1)
    go_right = go_right.at[1].set(0).at[2].set(MOVE).at[N_DP - 1].set(MOVE)
    go_left = go_left.at[3 % N_DP].set(0).at[2].set(MOVE).at[1].set(MOVE)
    from_lower = jnp.roll(go_right, 1)
    from_upper = jnp.roll(go_left, -1)
    keep_count = SLOTS_OUT - from_lower - from_upper
    live_count = keep_count + go_right + go_left
    lower_perm = jax.vmap(lambda k: jax.random.permutation(k, MOVE))(jax.random.split(subkeys[2], N_DP))
    upper_perm = jax.vmap(lambda k: jax.random.permutation(k, MOVE))(jax.random.split(subkeys[3], N_DP))
    positions = jax.vmap(lambda k: jax.random.permutation(k, SLOTS_IN))(jax.random.split(subkeys[4], N_DP))
    slot_ids = jnp.arange(SLOTS_IN, dtype=jnp.int32)[None, :]
    device_ids = jnp.arange(N_DP, dtype=jnp.int32)[:, None]
    free_lower = (MOVE - from_lower)[:, None]
    lower_index = jnp.clip(from_lower[:, None] + slot_ids, 0, MOVE - 1)
    upper_index = jnp.clip(from_upper[:, None] + slot_ids - free_lower, 0, MOVE - 1)
    keep_slot = jnp.where(slot_ids < free_lower, jnp.take_along_axis(lower_perm, lower_index, 1), MOVE + jnp.take_along_axis(upper_perm, upper_index, 1))
    right_index = jnp.clip(slot_ids - keep_count[:, None], 0, MOVE - 1)
    right_slot = jnp.take_along_axis(jnp.roll(lower_perm, -1, axis=0), right_index, 1)
    left_index = jnp.clip(slot_ids - keep_count[:, None] - go_right[:, None], 0, MOVE - 1)
    left_slot = MOVE + jnp.take_along_axis(jnp.roll(upper_perm, 1, axis=0), left_index, 1)
    is_keep = slot_ids < keep_count[:, None]
    is_right = slot_ids < (keep_count + go_right)[:, None]
    is_live = slot_ids < live_count[:, None]
    rank = jnp.where(is_keep, device_ids, jnp.where(is_right, (device_ids + 1) % N_DP, jnp.where(is_live, (device_ids + N_DP - 1) % N_DP, -1)))
    slot = jnp.where(is_keep, keep_slot, jnp.where(is_right, right_slot, jnp.where(is_live, left_slot, -1)))
    tokens = jnp.minimum(jax.random.randint(subkeys[5], (N_DP, SLOTS_IN), 1, 2 * BLOCK), BLOCK)
    tokens = jnp.where(is_live, tokens, 0).at[2, 0].set(BLOCK)
    inverse = jnp.argsort(positions, axis=1)
    rank = jnp.take_along_axis(rank, inverse, 1).reshape(-1)
    slot = jnp.take_along_axis(slot, inverse, 1).reshape(-1)
    tokens = jnp.take_along_axis(tokens, inverse, 1).reshape(-1)
    return (rank, slot, tokens)


def draw_move_plan(key, part):
    rank, slot, tokens = build_plan(key)
    return jnp.stack([rank, slot], axis=1).astype(jnp.int32)


def draw_live_tokens(key, part):
    rank, slot, tokens = build_plan(key)
    return tokens.astype(jnp.int32)


def draw_query_of_row(key, part):
    key = jax.random.fold_in(key, 5)
    return (jax.random.permutation(key, QR) // RANK).astype(jnp.int32)


def level_of(stream_key, dims, shards, least, largest):
    gain = 1.0
    for dim, blocks in shards:
        draws = jax.random.uniform(jax.random.fold_in(jax.random.fold_in(stream_key, 6), dim), (blocks,), jnp.float32, least / len(shards), largest / len(shards))
        gain = gain * jnp.repeat(jnp.exp(draws), dims[dim] // blocks).reshape((-1,) + (1,) * (len(dims) - 1 - dim))
    return gain


def normal_values(rng, shape, scale, limit, cuts=(), kind=jnp.bfloat16):
    array = scale * jax.random.normal(rng, shape, jnp.float32)
    if cuts:
        array = array * level_of(rng, shape, cuts, -0.22, 0.18)
    return jnp.clip(array, -limit, limit).astype(kind)


def setup_inputs(seed: int = 0, part: int = 0) -> dict:
    arg_keys = jax.random.split(jax.random.key(seed), 8)
    part_splits = jax.random.split(jax.random.fold_in(arg_keys[7], part), 8)
    return {
        "activations": normal_values(part_splits[0], (TOKENS_IN, HID), 1.0, 6.0, ((0, 8), (1, 2))),
        "out_grads": normal_values(part_splits[1], (TOKENS_IN, D), 1.0, 6.0, ((0, 8), (1, 2))),
        "act_factor": normal_values(arg_keys[2], (QR, HID), (HID * RANK) ** -0.5, 0.009765625, ((0, 8), (1, 2))),
        "grad_factor": normal_values(arg_keys[3], (QR, D), (D * BLOCK) ** -0.5, 0.015625, ((0, 8), (1, 2))),
        "query_of_row": draw_query_of_row(jax.random.fold_in(arg_keys[7], 71), part),
        "live_tokens": draw_live_tokens(jax.random.fold_in(jax.random.fold_in(arg_keys[7], part), 71), part),
        "move_plan": draw_move_plan(jax.random.fold_in(jax.random.fold_in(arg_keys[7], part), 71), part),
    }


def reference(activations, out_grads, act_factor, grad_factor, query_of_row, live_tokens, move_plan):
    slot_count = live_tokens.shape[0]
    offsets = jnp.arange(BLOCK, dtype=jnp.int32)
    live_mask = (offsets[None, :] < live_tokens[:, None]).reshape(-1)
    masked_grads = jnp.where(live_mask[:, None], out_grads, jnp.zeros_like(out_grads))
    grad_proj = jnp.dot(masked_grads, grad_factor.T, preferred_element_type=jnp.float32)
    act_proj = jnp.dot(activations, act_factor.T, preferred_element_type=jnp.float32)
    slot_rows = (grad_proj * act_proj).reshape(slot_count, BLOCK, QR).sum(axis=1)
    query_onehot = (query_of_row[:, None] == jnp.arange(QUERIES, dtype=jnp.int32)[None, :]).astype(jnp.float32)
    slot_scores = jnp.dot(slot_rows, query_onehot, precision=lax.Precision.HIGHEST, preferred_element_type=jnp.float32)
    target = move_plan[:, 0] * SLOTS_OUT + move_plan[:, 1]
    target = jnp.where(move_plan[:, 0] >= 0, target, N_DP * SLOTS_OUT).astype(jnp.int32)
    influence = jnp.zeros((N_DP * SLOTS_OUT, QUERIES), jnp.float32)
    return influence.at[target].set(slot_scores, mode="drop")
```

```python
import jax
import jax.numpy as jnp
from jax import lax
from jax.sharding import PartitionSpec as P

QUERIES = 20


def shifted(value, axis, steps):
    count = lax.axis_size(axis)
    pairs = [(source, (source + steps) % count) for source in range(count)]
    return lax.ppermute(value, axis, pairs)


def project_rows(rows, factor):
    return lax.dot_general(
        rows, factor, (((1,), (1,)), ((), ())), preferred_element_type=jnp.float32
    )


def swapped(value, axis):
    return lax.ppermute(value, axis, [(0, 1), (1, 0)])


def one_hot_queries(query_of_row):
    ids = jnp.arange(QUERIES, dtype=jnp.int32)[None, :]
    return (query_of_row[:, None] == ids).astype(jnp.float32)


def query_sums(rows, onehot):
    return jnp.dot(rows, onehot, precision=lax.Precision.HIGHEST, preferred_element_type=jnp.float32)


def gathered(activations, out_grads, act_factor, grad_factor, query_of_row, live_tokens, move_plan):
    slots_in = live_tokens.shape[0]
    block_len = activations.shape[0] // slots_in
    slots_out = slots_in // 2
    half_slots = slots_out // 2
    my_rank = lax.axis_index("dp")
    dp_size = lax.axis_size("dp")
    offsets = jnp.arange(block_len, dtype=jnp.int32)
    live_mask = (offsets[None, :] < live_tokens[:, None]).reshape(-1)
    grad_rows = jnp.where(live_mask[:, None], out_grads, jnp.zeros_like(out_grads))
    grad_all = lax.all_gather(grad_factor, "dp", axis=0, tiled=True)
    act_all = lax.all_gather(act_factor, "dp", axis=0, tiled=True)
    proj_grad = project_rows(grad_rows, grad_all)
    proj_act = project_rows(activations, act_all)
    full_grad, full_act = lax.psum((proj_grad, proj_act), "tensor")
    per_block = (full_grad * full_act).reshape(slots_in, block_len, -1).sum(axis=1)
    slot_scores = query_sums(per_block, one_hot_queries(query_of_row))
    keep, right, left = plan_weights(move_plan, my_rank, dp_size, slots_out, half_slots)
    lower = shifted(pick(right, slot_scores), "dp", 1)
    upper = shifted(pick(left, slot_scores), "dp", -1)
    return pick(keep, slot_scores) + jnp.concatenate([lower, upper], axis=0)


def plan_weights(move_plan, my_rank, dp_size, slots_out, half_slots):
    dest_rank = move_plan[:, 0]
    dest_slot = move_plan[:, 1]
    out_ids = jnp.arange(slots_out, dtype=jnp.int32)[:, None]
    hand_ids = jnp.arange(half_slots, dtype=jnp.int32)[:, None]
    keep = (dest_rank == my_rank)[None, :] & (dest_slot[None, :] == out_ids)
    right = (dest_rank == (my_rank + 1) % dp_size)[None, :] & (dest_slot[None, :] == hand_ids)
    left = (dest_rank == (my_rank + dp_size - 1) % dp_size)[None, :] & (
        dest_slot[None, :] == hand_ids + half_slots
    )
    return keep, right, left


def pick(hits, scores):
    return jnp.where(hits[:, :, None], scores[None, :, :], 0.0).sum(axis=1)


def ring_place(index, count):
    return jnp.where(index % 2 == 0, index // 2, count - 1 - index // 2)


def ring_index(place, count):
    place = place % count
    return jnp.where(place < count // 2, 2 * place, 2 * (count - 1 - place) + 1)


def ringed(activations, out_grads, act_factor, grad_factor, query_of_row, live_tokens, move_plan):
    dp_size = lax.axis_size("dp")
    my_rank = lax.axis_index("dp")
    group = lax.axis_index("groups")
    core = lax.axis_index("tensor")
    slots_in = live_tokens.shape[0]
    tokens, act_width = activations.shape
    grad_width = out_grads.shape[1]
    factor_rows = act_factor.shape[0]
    block_len = tokens // slots_in
    slots_out = slots_in // 2
    half_slots = slots_out // 2
    half_tokens = tokens // 2
    my_slots = slots_in // 2
    act_half, grad_half = act_width // 2, grad_width // 2

    def halves(acts, grads, side):
        act_part = lax.dynamic_slice_in_dim(acts, side * act_half, act_half, 1)
        grad_part = lax.dynamic_slice_in_dim(grads, side * grad_half, grad_half, 1)
        return jnp.concatenate([act_part, grad_part], axis=1)

    order = list(range(0, dp_size, 2)) + list(range(dp_size - 1, 0, -2))
    ahead = [(order[i], order[(i + 1) % dp_size]) for i in range(dp_size)]
    back = [(b, a) for a, b in ahead]

    def send_ahead(value):
        return lax.ppermute(value, "dp", ahead)

    def send_back(value):
        return lax.ppermute(value, "dp", back)

    own_factor = halves(act_factor, grad_factor, group)
    from_back, from_ahead = [own_factor], [own_factor]
    steps = dp_size // 2
    for _ in range(steps - 1):
        from_back.append(send_ahead(from_back[-1]))
        from_ahead.append(send_back(from_ahead[-1]))
    cut = factor_rows // 2
    last_factor = jnp.concatenate(
        [send_ahead(from_back[-1][:cut]), send_back(from_ahead[-1][cut:])], axis=0
    )

    def of_core(value, side):
        return lax.dynamic_slice_in_dim(value, side * half_tokens, half_tokens, 0)

    acts_keep, acts_give = of_core(activations, core), of_core(activations, 1 - core)
    grads_keep, grads_give = of_core(out_grads, core), of_core(out_grads, 1 - core)
    other = jnp.concatenate(
        [halves(acts_keep, grads_keep, 1 - group), halves(acts_give, grads_give, 1 - group)], axis=0
    )
    other = swapped(other, "groups")
    keep = jnp.concatenate([halves(acts_keep, grads_keep, group), other[:half_tokens]], axis=0)
    give = jnp.concatenate([halves(acts_give, grads_give, group), other[half_tokens:]], axis=0)

    place = ring_place(my_rank, dp_size)

    def onehot_of(distance):
        start = ring_index(place + distance, dp_size) * factor_rows
        return one_hot_queries(lax.dynamic_slice_in_dim(query_of_row, start, factor_rows, 0))

    live = lax.dynamic_slice_in_dim(live_tokens, core * my_slots, my_slots, 0)
    offsets = jnp.arange(block_len, dtype=jnp.int32)
    live_mask = (offsets[None, :] < live[:, None])[:, :, None]

    def scores_of(act, grad, onehot):
        product = (act * grad).reshape(my_slots, block_len, -1)
        return query_sums(jnp.where(live_mask, product, 0.0).sum(axis=1), onehot)

    def project(rows, factor):
        return (
            project_rows(rows[:, :act_half], factor[:, :act_half]),
            project_rows(rows[:, act_half:], factor[:, act_half:]),
        )

    own_act = project_rows(acts_keep, act_factor) + swapped(project_rows(acts_give, act_factor), "tensor")
    own_grad = project_rows(grads_keep, grad_factor) + swapped(
        project_rows(grads_give, grad_factor), "tensor"
    )
    scores = scores_of(own_act, own_grad, onehot_of(0))

    def shared_scores(factor, onehot):
        given_act, given_grad = project(give, factor)
        got_act, got_grad = swapped(given_act, "tensor"), swapped(given_grad, "tensor")
        kept_act, kept_grad = project(keep, factor)
        act, grad = kept_act + got_act, kept_grad + got_grad
        act = act[:half_tokens] + swapped(act[half_tokens:], "groups")
        grad = grad[:half_tokens] + swapped(grad[half_tokens:], "groups")
        return scores_of(act, grad, onehot)

    early, early_onehot = [], []
    for distance in range(1, steps):
        early += [from_back[distance], from_ahead[distance]]
        early_onehot += [onehot_of(-distance), onehot_of(distance)]
    scores += shared_scores(jnp.concatenate(early, axis=0), jnp.concatenate(early_onehot, axis=0))
    scores += shared_scores(last_factor, onehot_of(steps))

    my_plan = lax.dynamic_slice_in_dim(move_plan, core * my_slots, my_slots, 0)
    keep_hits, right_hits, left_hits = plan_weights(my_plan, my_rank, dp_size, slots_out, half_slots)
    own, right, left = pick(keep_hits, scores), pick(right_hits, scores), pick(left_hits, scores)

    def across(value, steps):
        pairs = [
            (2 * source + side, 2 * ((source + steps) % dp_size) + 1 - side)
            for source in range(dp_size)
            for side in range(2)
        ]
        return lax.ppermute(value, ("dp", "tensor"), pairs)

    own += swapped(own, "tensor")
    lower = shifted(right, "dp", 1) + across(right, 1)
    upper = shifted(left, "dp", -1) + across(left, -1)
    return own + jnp.concatenate([lower, upper], axis=0)


def solution(mesh):
    paired = mesh.shape["groups"] == 2 and mesh.shape["tensor"] == 2
    short = mesh.shape["dp"] % 2 == 0 and 4 <= mesh.shape["dp"] <= 16
    return jax.shard_map(
        ringed if paired and short else gathered,
        mesh=mesh,
        in_specs=(
            P(("groups", "dp"), "tensor"),
            P(("groups", "dp"), "tensor"),
            P("dp", "tensor"),
            P("dp", "tensor"),
            P(),
            P(("groups", "dp")),
            P(("groups", "dp"), None),
        ),
        out_specs=P(("groups", "dp"), None),
        check_vma=False,
    )
```

```python
import functools

import jax
import jax.numpy as jnp
from jax import lax
from jax.experimental import pallas as pl
from jax.experimental.pallas import tpu as pltpu
from jax.sharding import PartitionSpec as P

QUERIES = 20


def shifted(value, axis, steps):
    count = lax.axis_size(axis)
    pairs = [(source, (source + steps) % count) for source in range(count)]
    return lax.ppermute(value, axis, pairs)


def project_rows(rows, factor):
    return lax.dot_general(
        rows, factor, (((1,), (1,)), ((), ())), preferred_element_type=jnp.float32
    )


def swapped(value, axis):
    return lax.ppermute(value, axis, [(0, 1), (1, 0)])


def one_hot_queries(query_of_row):
    ids = jnp.arange(QUERIES, dtype=jnp.int32)[None, :]
    return (query_of_row[:, None] == ids).astype(jnp.float32)


def query_sums(rows, onehot):
    return jnp.dot(rows, onehot, precision=lax.Precision.HIGHEST, preferred_element_type=jnp.float32)


def gathered(activations, out_grads, act_factor, grad_factor, query_of_row, live_tokens, move_plan):
    slots_in = live_tokens.shape[0]
    block_len = activations.shape[0] // slots_in
    slots_out = slots_in // 2
    half_slots = slots_out // 2
    my_rank = lax.axis_index("dp")
    dp_size = lax.axis_size("dp")
    offsets = jnp.arange(block_len, dtype=jnp.int32)
    live_mask = (offsets[None, :] < live_tokens[:, None]).reshape(-1)
    grad_rows = jnp.where(live_mask[:, None], out_grads, jnp.zeros_like(out_grads))
    grad_all = lax.all_gather(grad_factor, "dp", axis=0, tiled=True)
    act_all = lax.all_gather(act_factor, "dp", axis=0, tiled=True)
    proj_grad = project_rows(grad_rows, grad_all)
    proj_act = project_rows(activations, act_all)
    full_grad, full_act = lax.psum((proj_grad, proj_act), "tensor")
    per_block = (full_grad * full_act).reshape(slots_in, block_len, -1).sum(axis=1)
    slot_scores = query_sums(per_block, one_hot_queries(query_of_row))
    keep, right, left = plan_weights(move_plan, my_rank, dp_size, slots_out, half_slots)
    lower = shifted(pick(right, slot_scores), "dp", 1)
    upper = shifted(pick(left, slot_scores), "dp", -1)
    return pick(keep, slot_scores) + jnp.concatenate([lower, upper], axis=0)


def plan_weights(move_plan, my_rank, dp_size, slots_out, half_slots):
    dest_rank = move_plan[:, 0]
    dest_slot = move_plan[:, 1]
    out_ids = jnp.arange(slots_out, dtype=jnp.int32)[:, None]
    hand_ids = jnp.arange(half_slots, dtype=jnp.int32)[:, None]
    keep = (dest_rank == my_rank)[None, :] & (dest_slot[None, :] == out_ids)
    right = (dest_rank == (my_rank + 1) % dp_size)[None, :] & (dest_slot[None, :] == hand_ids)
    left = (dest_rank == (my_rank + dp_size - 1) % dp_size)[None, :] & (
        dest_slot[None, :] == hand_ids + half_slots
    )
    return keep, right, left


def pick(hits, scores):
    return jnp.where(hits[:, :, None], scores[None, :, :], 0.0).sum(axis=1)


def ring_place(index, count):
    step = lax.div(index, 2)
    return jnp.where(lax.rem(index, 2) == 0, step, count - 1 - step)


def ring_index(place, count):
    place = lax.rem(place, count)
    return jnp.where(place < count // 2, 2 * place, 2 * (count - 1 - place) + 1)


LANES = 128
SUBLANES = 16
QUERY_LANES = 32
DEST_ROWS = 8


def after(value, *others):
    return lax.optimization_barrier((value, *others))[0]


def kernel_call(body, out_shape, in_specs, out_specs, operands, scratch=(), flops=0, limit=24):
    return pl.pallas_call(
        body,
        out_shape=out_shape,
        in_specs=in_specs,
        out_specs=out_specs,
        scratch_shapes=list(scratch),
        compiler_params=pltpu.CompilerParams(vmem_limit_bytes=limit * 1024 * 1024),
        cost_estimate=pl.CostEstimate(flops=flops, bytes_accessed=0, transcendentals=0),
    )(*operands)


def dot_rows(left, right):
    return lax.dot_general(
        left, right, (((1,), (1,)), ((), ())), preferred_element_type=jnp.float32
    )


def halves_kernel(acts, grads, act_factor, grad_factor, first, second, other, sems):
    act_half, grad_half = acts.shape[1] // 2, grads.shape[1] // 2
    cut = first.shape[1]
    group = lax.axis_index("groups")

    def columns(side, width, skip=0, size=None):
        return pl.ds(pl.multiple_of(side * width + skip, LANES), width if size is None else size)

    moves = [
        (act_factor.at[:, columns(group, act_half, 0, cut)], first),
        (act_factor.at[:, columns(group, act_half, cut, act_half - cut)], second.at[:, pl.ds(0, act_half - cut)]),
        (grad_factor.at[:, columns(group, grad_half)], second.at[:, pl.ds(act_half - cut, grad_half)]),
    ]
    size = acts.shape[0] // 4
    for part in range(4):
        some = pl.ds(part * size, size)
        moves += [
            (acts.at[some, columns(1 - group, act_half)], other.at[some, pl.ds(0, act_half)]),
            (grads.at[some, columns(1 - group, grad_half)], other.at[some, pl.ds(act_half, grad_half)]),
        ]
    copies = [pltpu.make_async_copy(src, dst, sems.at[i]) for i, (src, dst) in enumerate(moves)]
    for copy in copies:
        copy.start()
    for copy in copies:
        copy.wait()


def split_cores(act, grad, give, keep, sums, start):
    rows = act.shape[1]
    tokens = sums.shape[0]
    core = lax.axis_index("tensor")
    for i, value in enumerate((act, grad)):
        sums[:, :rows] = value
        for out, side in ((give, 1 - core), (keep, core)):
            some = sums[pl.ds(pl.multiple_of(side * (tokens // 2), LANES), tokens // 2), :]
            out[start + i * rows : start + (i + 1) * rows, :] = some.T[:rows]


def own_rows_kernel(acts, grads, act_factor, grad_factor, give, keep, own, sums):
    act_half, grad_half = acts.shape[1] // 2, grads.shape[1] // 2
    group = lax.axis_index("groups")
    act = dot_rows(acts[...], act_factor[...])
    grad = dot_rows(grads[...], grad_factor[...])
    split_cores(act, grad, give, keep, sums, 0)
    own[:, :act_half] = acts[:, pl.ds(pl.multiple_of(group * act_half, LANES), act_half)]
    own[:, act_half:] = grads[:, pl.ds(pl.multiple_of(group * grad_half, LANES), grad_half)]


def near_own_kernel(count, act_half, tokens, *refs):
    pieces, (factor, give, keep, sums, sems) = refs[:count], refs[count:]
    rows, cut = pieces[0].shape
    copies = []
    for i, piece in enumerate(pieces):
        columns = pl.ds(0, cut) if i % 2 == 0 else pl.ds(cut, factor.shape[1] - cut)
        copies.append(
            pltpu.make_async_copy(piece, factor.at[pl.ds(i // 2 * rows, rows), columns], sems.at[i])
        )
    for copy in copies:
        copy.start()
    for copy in copies:
        copy.wait()
    near_other_kernel(act_half, tokens, factor, give, keep, sums)


def near_other_kernel(act_half, tokens, factor, give, keep, sums):
    act = dot_rows(tokens[:, :act_half], factor[:, :act_half])
    grad = dot_rows(tokens[:, act_half:], factor[:, act_half:])
    split_cores(act, grad, give, keep, sums, 0)


def last_kernel(act_half, own, other, first, second, give, keep, sums):
    rows, cut = first.shape
    rest = act_half - cut
    for i, tokens in enumerate((own, other)):
        act = dot_rows(tokens[:, :cut], first[...]) + dot_rows(tokens[:, cut:act_half], second[:, :rest])
        grad = dot_rows(tokens[:, act_half:], second[:, rest:])
        split_cores(act, grad, give, keep, sums, 2 * rows * i)


def scores_kernel(block_len, dp_size, live_tokens, move_plan, query, *refs):
    exact = functools.partial(
        lax.dot_general, precision=lax.Precision.HIGHEST, preferred_element_type=jnp.float32
    )
    sets, out = refs[:-1], refs[-1]
    rows = sets[0].shape[0] // 2
    products = []
    for terms in (sets[:2], sets[2:5], sets[5:8], sets[8:]):
        size = terms[-1].shape[0]
        total = sum(term[:size, :] for term in terms)
        products.append(total[: size // 2] * total[size // 2 :])
    product = jnp.concatenate(products, axis=0)
    my_rank = lax.axis_index("dp")
    place = ring_place(my_rank, dp_size)
    distances = [0]
    for distance in range(1, dp_size // 2):
        distances += [-distance, distance]
    distances.append(dp_size // 2)
    ids = lax.broadcasted_iota(jnp.int32, (rows, QUERY_LANES), 1)
    onehots = []
    for distance in distances:
        start = ring_index(place + distance + dp_size, dp_size) * rows
        onehots.append((query[pl.ds(pl.multiple_of(start, 8), rows), :] == ids).astype(jnp.float32))
    sums = exact(jnp.concatenate(onehots, axis=0), product, (((0,), (0,)), ((), ())))
    tokens = sums.shape[1]
    slots = tokens // block_len
    token = lax.broadcasted_iota(jnp.int32, (3 * DEST_ROWS, tokens), 1)
    dest = lax.broadcasted_iota(jnp.int32, (3 * DEST_ROWS, tokens), 0)
    moves = jnp.zeros((3 * DEST_ROWS, tokens), jnp.float32)
    right = jnp.where(my_rank == dp_size - 1, 0, my_rank + 1)
    for slot in range(slots):
        mine = lax.axis_index("tensor") * slots + slot
        rank = move_plan[mine, 0]
        side = jnp.where(rank == my_rank, 0, jnp.where(rank == right, 1, 2))
        target = jnp.where(rank >= 0, side * DEST_ROWS + move_plan[mine, 1], -1)
        start = slot * block_len
        hit = (token >= start) & (token < start + live_tokens[mine]) & (dest == target)
        moves = moves + hit.astype(jnp.float32)
    out[...] = exact(moves, sums, (((1,), (1,)), ((), ())))


def ringed(activations, out_grads, act_factor, grad_factor, query_of_row, live_tokens, move_plan):
    dp_size = lax.axis_size("dp")
    slots_in = live_tokens.shape[0]
    tokens, act_width = activations.shape
    grad_width = out_grads.shape[1]
    rows = act_factor.shape[0]
    block_len = tokens // slots_in
    slots_out = slots_in // 2
    half = tokens // 2
    act_half, grad_half = act_width // 2, grad_width // 2
    width = act_half + grad_half
    cut = (width // 2) // LANES * LANES
    steps = dp_size // 2
    any_space = pl.BlockSpec(memory_space=pl.ANY)
    whole = pl.BlockSpec(memory_space=pltpu.VMEM)
    bf16, f32 = jnp.bfloat16, jnp.float32

    order = list(range(0, dp_size, 2)) + list(range(dp_size - 1, 0, -2))
    ahead = [(order[i], order[(i + 1) % dp_size]) for i in range(dp_size)]
    back = [(b, a) for a, b in ahead]
    smem = pl.BlockSpec(memory_space=pltpu.SMEM)

    first, second, other = kernel_call(
        halves_kernel,
        [
            jax.ShapeDtypeStruct((rows, cut), bf16),
            jax.ShapeDtypeStruct((rows, width - cut), bf16),
            jax.ShapeDtypeStruct((tokens, width), bf16),
        ],
        [any_space] * 4,
        [whole] * 3,
        (activations, out_grads, act_factor, grad_factor),
        scratch=[pltpu.SemaphoreType.DMA((11,))],
        limit=60,
    )
    other = swapped(other, "groups")

    def sent(pieces, pairs):
        return tuple(lax.ppermute(piece, "dp", pairs) for piece in pieces)

    start = (first, second)
    from_back, from_ahead = [start, sent(start, ahead)], [start, sent(start, back)]
    from_back.append(sent(from_back[1], ahead))
    from_ahead.append(sent(from_ahead[1], back))

    def work(factor_rows, features):
        return 2 * factor_rows * tokens * features

    halves = [jax.ShapeDtypeStruct((2 * rows, half), f32)] * 2
    sums = pltpu.VMEM((tokens, LANES), f32)
    own_give, own_keep, own = kernel_call(
        own_rows_kernel,
        halves + [jax.ShapeDtypeStruct((tokens, width), bf16)],
        [whole] * 4,
        [whole] * 3,
        lax.optimization_barrier(
            (activations, out_grads, act_factor, grad_factor, *from_back[1], *from_ahead[1])
        )[:4],
        scratch=[sums],
        flops=work(rows, 2 * width),
    )
    own_got = swapped(own_give, "tensor")

    def tied(pieces, *others):
        return lax.optimization_barrier((*pieces, *others))[: len(pieces)]

    def wide_sums(count):
        return pltpu.VMEM((tokens, -(-count // LANES) * LANES), f32)

    def against_own(pieces):
        count = rows * len(pieces) // 2
        factor, give, keep = kernel_call(
            functools.partial(near_own_kernel, len(pieces), act_half),
            [jax.ShapeDtypeStruct((count, width), bf16)] + [jax.ShapeDtypeStruct((2 * count, half), f32)] * 2,
            [whole] + [any_space] * len(pieces),
            [whole] * 3,
            (own, *pieces),
            scratch=[wide_sums(count), pltpu.SemaphoreType.DMA((len(pieces),))],
            flops=work(count, width),
        )
        return factor, give, keep, swapped(give, "tensor")

    def against_other(factor, other):
        count = factor.shape[0]
        give, keep = kernel_call(
            functools.partial(near_other_kernel, act_half),
            [jax.ShapeDtypeStruct((2 * count, half), f32)] * 2,
            [whole] * 2,
            [whole] * 2,
            (other, factor),
            scratch=[wide_sums(count)],
            flops=work(count, width),
        )
        return swapped(keep + swapped(give, "tensor"), "groups"), keep

    for distance in range(2, steps - 2):
        from_back.append(sent(from_back[distance], ahead))
        from_ahead.append(sent(from_ahead[distance], back))
    from_back.append(sent(tied(from_back[steps - 2], own_give), ahead))
    from_ahead.append(sent(tied(from_ahead[steps - 2], own_give), back))
    near_pieces = []
    for distance in range(1, steps - 1):
        near_pieces += [*from_back[distance], *from_ahead[distance]]
    near, near_give, near_keep, near_got = against_own(near_pieces)
    far_pieces = [*from_back[steps - 1], *from_ahead[steps - 1]]
    last_first, last_second = tied((from_back[-1][0], from_ahead[-1][1]), near_give)
    last = [lax.ppermute(last_first, "dp", ahead), lax.ppermute(last_second, "dp", back)]
    far, far_give, far_keep, far_got = against_own(far_pieces)
    other = after(other, far)
    near_other, near_done = against_other(near, other)
    far_other, _ = against_other(far, after(other, near_done))

    last_give, last_keep = kernel_call(
        functools.partial(last_kernel, act_half),
        [jax.ShapeDtypeStruct((4 * rows, half), f32)] * 2,
        [whole] * 4,
        [whole] * 2,
        (own, other, *last),
        scratch=[sums],
        flops=16 * 2 * work(rows, width),
    )
    last_got = swapped(last_give, "tensor")
    last_other = swapped(last_keep[2 * rows :] + last_got[2 * rows :], "groups")

    moved = kernel_call(
        functools.partial(scores_kernel, block_len, dp_size),
        jax.ShapeDtypeStruct((3 * DEST_ROWS, QUERY_LANES), f32),
        [smem, smem] + [whole] * 12,
        whole,
        (live_tokens, move_plan, query_of_row.reshape(-1, 1), own_keep, own_got, near_keep, near_got,
         near_other, far_keep, far_got, far_other, last_keep, last_got, last_other),
    )
    moved = moved + swapped(moved, "tensor")
    kept, right, left = (moved[i * DEST_ROWS : (i + 1) * DEST_ROWS] for i in range(3))
    total = kept + shifted(right, "dp", 1) + shifted(left, "dp", -1)
    return total[:slots_out, :QUERIES]


def shards(activations, out_grads, act_factor, grad_factor, query_of_row, live_tokens, move_plan):
    args = (activations, out_grads, act_factor, grad_factor, query_of_row, live_tokens, move_plan)
    dp_size = lax.axis_size("dp")
    tokens, act_width = activations.shape
    grad_width = out_grads.shape[1]
    rows = act_factor.shape[0]
    slots_in = live_tokens.shape[0]
    fits = (
        lax.axis_size("groups") == 2
        and lax.axis_size("tensor") == 2
        and dp_size % 2 == 0
        and 6 <= dp_size <= 16
        and act_width % (2 * LANES) == 0
        and grad_width % (2 * LANES) == 0
        and tokens == 2 * LANES
        and rows % SUBLANES == 0
        and slots_in % 4 == 0
        and slots_in <= 2 * DEST_ROWS
    )
    return ringed(*args) if fits else gathered(*args)


def solution(mesh):
    return jax.shard_map(
        shards,
        mesh=mesh,
        in_specs=(
            P(("groups", "dp"), "tensor"),
            P(("groups", "dp"), "tensor"),
            P("dp", "tensor"),
            P("dp", "tensor"),
            P(),
            P(("groups", "dp")),
            P(("groups", "dp"), None),
        ),
        out_specs=P(("groups", "dp"), None),
        check_vma=False,
    )
```

```python
import functools

import jax
import jax.numpy as jnp
from jax import lax
from jax.experimental import pallas as pl
from jax.experimental.pallas import tpu as pltpu
from jax.sharding import PartitionSpec as P

QUERIES = 20


def shifted(value, axis, steps):
    count = lax.axis_size(axis)
    pairs = [(source, (source + steps) % count) for source in range(count)]
    return lax.ppermute(value, axis, pairs)


def project_rows(rows, factor):
    return lax.dot_general(
        rows, factor, (((1,), (1,)), ((), ())), preferred_element_type=jnp.float32
    )


def swapped(value, axis):
    return lax.ppermute(value, axis, [(0, 1), (1, 0)])


def one_hot_queries(query_of_row):
    ids = jnp.arange(QUERIES, dtype=jnp.int32)[None, :]
    return (query_of_row[:, None] == ids).astype(jnp.float32)


def query_sums(rows, onehot):
    return jnp.dot(rows, onehot, precision=lax.Precision.HIGHEST, preferred_element_type=jnp.float32)


def gathered(activations, out_grads, act_factor, grad_factor, query_of_row, live_tokens, move_plan):
    slots_in = live_tokens.shape[0]
    block_len = activations.shape[0] // slots_in
    slots_out = slots_in // 2
    half_slots = slots_out // 2
    my_rank = lax.axis_index("dp")
    dp_size = lax.axis_size("dp")
    offsets = jnp.arange(block_len, dtype=jnp.int32)
    live_mask = (offsets[None, :] < live_tokens[:, None]).reshape(-1)
    grad_rows = jnp.where(live_mask[:, None], out_grads, jnp.zeros_like(out_grads))
    grad_all = lax.all_gather(grad_factor, "dp", axis=0, tiled=True)
    act_all = lax.all_gather(act_factor, "dp", axis=0, tiled=True)
    proj_grad = project_rows(grad_rows, grad_all)
    proj_act = project_rows(activations, act_all)
    full_grad, full_act = lax.psum((proj_grad, proj_act), "tensor")
    per_block = (full_grad * full_act).reshape(slots_in, block_len, -1).sum(axis=1)
    slot_scores = query_sums(per_block, one_hot_queries(query_of_row))
    keep, right, left = plan_weights(move_plan, my_rank, dp_size, slots_out, half_slots)
    lower = shifted(pick(right, slot_scores), "dp", 1)
    upper = shifted(pick(left, slot_scores), "dp", -1)
    return pick(keep, slot_scores) + jnp.concatenate([lower, upper], axis=0)


def plan_weights(move_plan, my_rank, dp_size, slots_out, half_slots):
    dest_rank = move_plan[:, 0]
    dest_slot = move_plan[:, 1]
    out_ids = jnp.arange(slots_out, dtype=jnp.int32)[:, None]
    hand_ids = jnp.arange(half_slots, dtype=jnp.int32)[:, None]
    keep = (dest_rank == my_rank)[None, :] & (dest_slot[None, :] == out_ids)
    right = (dest_rank == (my_rank + 1) % dp_size)[None, :] & (dest_slot[None, :] == hand_ids)
    left = (dest_rank == (my_rank + dp_size - 1) % dp_size)[None, :] & (
        dest_slot[None, :] == hand_ids + half_slots
    )
    return keep, right, left


def pick(hits, scores):
    return jnp.where(hits[:, :, None], scores[None, :, :], 0.0).sum(axis=1)


def ring_place(index, count):
    step = lax.div(index, 2)
    return jnp.where(lax.rem(index, 2) == 0, step, count - 1 - step)


def ring_index(place, count):
    place = lax.rem(place, count)
    return jnp.where(place < count // 2, 2 * place, 2 * (count - 1 - place) + 1)


LANES = 128
SUBLANES = 16
QUERY_LANES = 32
DEST_ROWS = 8


def after(value, *others):
    return lax.optimization_barrier((value, *others))[0]


def kernel_call(body, out_shape, in_specs, out_specs, operands, scratch=(), flops=0, limit=24):
    return pl.pallas_call(
        body,
        out_shape=out_shape,
        in_specs=in_specs,
        out_specs=out_specs,
        scratch_shapes=list(scratch),
        compiler_params=pltpu.CompilerParams(vmem_limit_bytes=limit * 1024 * 1024),
        cost_estimate=pl.CostEstimate(flops=flops, bytes_accessed=0, transcendentals=0),
    )(*operands)


def dot_rows(left, right):
    return lax.dot_general(
        left, right, (((1,), (1,)), ((), ())), preferred_element_type=jnp.float32
    )


def halves_kernel(acts, grads, act_factor, grad_factor, first, second, other, sems):
    act_half, grad_half = acts.shape[1] // 2, grads.shape[1] // 2
    cut = first.shape[1]
    group = lax.axis_index("groups")

    def columns(side, width, skip=0, size=None):
        return pl.ds(pl.multiple_of(side * width + skip, LANES), width if size is None else size)

    moves = [
        (act_factor.at[:, columns(group, act_half, 0, cut)], first),
        (act_factor.at[:, columns(group, act_half, cut, act_half - cut)], second.at[:, pl.ds(0, act_half - cut)]),
        (grad_factor.at[:, columns(group, grad_half)], second.at[:, pl.ds(act_half - cut, grad_half)]),
    ]
    size = acts.shape[0] // 4
    for part in range(4):
        some = pl.ds(part * size, size)
        moves += [
            (acts.at[some, columns(1 - group, act_half)], other.at[some, pl.ds(0, act_half)]),
            (grads.at[some, columns(1 - group, grad_half)], other.at[some, pl.ds(act_half, grad_half)]),
        ]
    copies = [pltpu.make_async_copy(src, dst, sems.at[i]) for i, (src, dst) in enumerate(moves)]
    for copy in copies:
        copy.start()
    for copy in copies:
        copy.wait()


def split_cores(act, grad, give, keep, sums, start):
    rows = act.shape[1]
    tokens = sums.shape[0]
    core = lax.axis_index("tensor")
    for i, value in enumerate((act, grad)):
        sums[:, :rows] = value
        for out, side in ((give, 1 - core), (keep, core)):
            some = sums[pl.ds(pl.multiple_of(side * (tokens // 2), LANES), tokens // 2), :]
            out[start + i * rows : start + (i + 1) * rows, :] = some.T[:rows]


def own_rows_kernel(acts, grads, act_factor, grad_factor, give, keep, own, sums):
    act_half, grad_half = acts.shape[1] // 2, grads.shape[1] // 2
    group = lax.axis_index("groups")
    act = dot_rows(acts[...], act_factor[...])
    grad = dot_rows(grads[...], grad_factor[...])
    split_cores(act, grad, give, keep, sums, 0)
    own[:, :act_half] = acts[:, pl.ds(pl.multiple_of(group * act_half, LANES), act_half)]
    own[:, act_half:] = grads[:, pl.ds(pl.multiple_of(group * grad_half, LANES), grad_half)]


def near_own_kernel(count, act_half, tokens, *refs):
    pieces, (factor, give, keep, sums, sems) = refs[:count], refs[count:]
    rows, cut = pieces[0].shape
    copies = []
    for i, piece in enumerate(pieces):
        columns = pl.ds(0, cut) if i % 2 == 0 else pl.ds(cut, factor.shape[1] - cut)
        copies.append(
            pltpu.make_async_copy(piece, factor.at[pl.ds(i // 2 * rows, rows), columns], sems.at[i])
        )
    for copy in copies:
        copy.start()
    for copy in copies:
        copy.wait()
    near_other_kernel(act_half, tokens, factor, give, keep, sums)


def near_other_kernel(act_half, tokens, factor, give, keep, sums):
    act = dot_rows(tokens[:, :act_half], factor[:, :act_half])
    grad = dot_rows(tokens[:, act_half:], factor[:, act_half:])
    split_cores(act, grad, give, keep, sums, 0)


def last_kernel(act_half, own, other, first, second, give, keep, sums):
    rows, cut = first.shape
    rest = act_half - cut
    for i, tokens in enumerate((own, other)):
        act = dot_rows(tokens[:, :cut], first[...]) + dot_rows(tokens[:, cut:act_half], second[:, :rest])
        grad = dot_rows(tokens[:, act_half:], second[:, rest:])
        split_cores(act, grad, give, keep, sums, 2 * rows * i)


def scores_kernel(block_len, dp_size, live_tokens, move_plan, query, *refs):
    exact = functools.partial(
        lax.dot_general, precision=lax.Precision.HIGHEST, preferred_element_type=jnp.float32
    )
    sets, out = refs[:-1], refs[-1]
    rows = sets[0].shape[0] // 2
    products = []
    for terms in (sets[:2], sets[2:5], sets[5:8], sets[8:]):
        size = terms[-1].shape[0]
        total = sum(term[:size, :] for term in terms)
        products.append(total[: size // 2] * total[size // 2 :])
    product = jnp.concatenate(products, axis=0)
    my_rank = lax.axis_index("dp")
    place = ring_place(my_rank, dp_size)
    distances = [0]
    for distance in range(1, dp_size // 2):
        distances += [-distance, distance]
    distances.append(dp_size // 2)
    ids = lax.broadcasted_iota(jnp.int32, (rows, QUERY_LANES), 1)
    onehots = []
    for distance in distances:
        start = ring_index(place + distance + dp_size, dp_size) * rows
        onehots.append((query[pl.ds(pl.multiple_of(start, 8), rows), :] == ids).astype(jnp.float32))
    sums = exact(jnp.concatenate(onehots, axis=0), product, (((0,), (0,)), ((), ())))
    tokens = sums.shape[1]
    slots = tokens // block_len
    token = lax.broadcasted_iota(jnp.int32, (3 * DEST_ROWS, tokens), 1)
    dest = lax.broadcasted_iota(jnp.int32, (3 * DEST_ROWS, tokens), 0)
    moves = jnp.zeros((3 * DEST_ROWS, tokens), jnp.float32)
    odd = lax.rem(my_rank, 2)
    partner = jnp.where(odd == 1, my_rank + 1, my_rank - 1 + dp_size)
    partner = lax.rem(partner, dp_size)
    for slot in range(slots):
        mine = lax.axis_index("tensor") * slots + slot
        rank = move_plan[mine, 0]
        side = jnp.where(rank == my_rank, 0, jnp.where(rank == partner, 1, 2))
        target = jnp.where(rank >= 0, side * DEST_ROWS + move_plan[mine, 1], -1)
        start = slot * block_len
        hit = (token >= start) & (token < start + live_tokens[mine]) & (dest == target)
        moves = moves + hit.astype(jnp.float32)
    out[...] = exact(moves, sums, (((1,), (1,)), ((), ())))


def ringed(activations, out_grads, act_factor, grad_factor, query_of_row, live_tokens, move_plan):
    dp_size = lax.axis_size("dp")
    slots_in = live_tokens.shape[0]
    tokens, act_width = activations.shape
    grad_width = out_grads.shape[1]
    rows = act_factor.shape[0]
    block_len = tokens // slots_in
    slots_out = slots_in // 2
    half = tokens // 2
    act_half, grad_half = act_width // 2, grad_width // 2
    width = act_half + grad_half
    cut = (width // 2) // LANES * LANES
    steps = dp_size // 2
    any_space = pl.BlockSpec(memory_space=pl.ANY)
    whole = pl.BlockSpec(memory_space=pltpu.VMEM)
    bf16, f32 = jnp.bfloat16, jnp.float32

    order = list(range(0, dp_size, 2)) + list(range(dp_size - 1, 0, -2))
    ahead = [(order[i], order[(i + 1) % dp_size]) for i in range(dp_size)]
    back = [(b, a) for a, b in ahead]
    smem = pl.BlockSpec(memory_space=pltpu.SMEM)

    first, second, other = kernel_call(
        halves_kernel,
        [
            jax.ShapeDtypeStruct((rows, cut), bf16),
            jax.ShapeDtypeStruct((rows, width - cut), bf16),
            jax.ShapeDtypeStruct((tokens, width), bf16),
        ],
        [any_space] * 4,
        [whole] * 3,
        (activations, out_grads, act_factor, grad_factor),
        scratch=[pltpu.SemaphoreType.DMA((11,))],
        limit=60,
    )
    other = swapped(other, "groups")

    def sent(pieces, pairs):
        return tuple(lax.ppermute(piece, "dp", pairs) for piece in pieces)

    start = (first, second)
    from_back, from_ahead = [start, sent(start, ahead)], [start, sent(start, back)]
    from_back.append(sent(from_back[1], ahead))
    from_ahead.append(sent(from_ahead[1], back))

    def work(factor_rows, features):
        return 2 * factor_rows * tokens * features

    halves = [jax.ShapeDtypeStruct((2 * rows, half), f32)] * 2
    sums = pltpu.VMEM((tokens, LANES), f32)
    own_give, own_keep, own = kernel_call(
        own_rows_kernel,
        halves + [jax.ShapeDtypeStruct((tokens, width), bf16)],
        [whole] * 4,
        [whole] * 3,
        lax.optimization_barrier(
            (activations, out_grads, act_factor, grad_factor, *from_back[1], *from_ahead[1])
        )[:4],
        scratch=[sums],
        flops=work(rows, 2 * width),
    )
    own_got = swapped(own_give, "tensor")

    def tied(pieces, other):
        return [after(piece, other) for piece in pieces]

    def wide_sums(count):
        return pltpu.VMEM((tokens, -(-count // LANES) * LANES), f32)

    def against_own(pieces):
        count = rows * len(pieces) // 2
        factor, give, keep = kernel_call(
            functools.partial(near_own_kernel, len(pieces), act_half),
            [jax.ShapeDtypeStruct((count, width), bf16)] + [jax.ShapeDtypeStruct((2 * count, half), f32)] * 2,
            [whole] + [any_space] * len(pieces),
            [whole] * 3,
            (own, *pieces),
            scratch=[wide_sums(count), pltpu.SemaphoreType.DMA((len(pieces),))],
            flops=work(count, width),
        )
        return factor, give, keep, swapped(give, "tensor")

    def against_other(factor, other):
        count = factor.shape[0]
        give, keep = kernel_call(
            functools.partial(near_other_kernel, act_half),
            [jax.ShapeDtypeStruct((2 * count, half), f32)] * 2,
            [whole] * 2,
            [whole] * 2,
            (other, factor),
            scratch=[wide_sums(count)],
            flops=work(count, width),
        )
        return swapped(keep + swapped(give, "tensor"), "groups"), keep

    for distance in range(2, steps - 2):
        from_back.append(sent(from_back[distance], ahead))
        from_ahead.append(sent(from_ahead[distance], back))
    from_back.append(sent(tied(from_back[steps - 2], own_give), ahead))
    from_ahead.append(sent(tied(from_ahead[steps - 2], own_give), back))
    near_pieces = []
    for distance in range(1, steps - 1):
        near_pieces += [*from_back[distance], *from_ahead[distance]]
    near, near_give, near_keep, near_got = against_own(near_pieces)
    far_pieces = [*from_back[steps - 1], *from_ahead[steps - 1]]
    last_first, last_second = tied((from_back[-1][0], from_ahead[-1][1]), near_give)
    last = [lax.ppermute(last_first, "dp", ahead), lax.ppermute(last_second, "dp", back)]
    far, far_give, far_keep, far_got = against_own(far_pieces)
    other = after(other, far)
    near_other, near_done = against_other(near, other)
    far_other, _ = against_other(far, after(other, near_done))

    last_give, last_keep = kernel_call(
        functools.partial(last_kernel, act_half),
        [jax.ShapeDtypeStruct((4 * rows, half), f32)] * 2,
        [whole] * 4,
        [whole] * 2,
        (own, other, *last),
        scratch=[sums],
        flops=16 * 2 * work(rows, width),
    )
    last_got = swapped(last_give, "tensor")
    last_other = swapped(last_keep[2 * rows :] + last_got[2 * rows :], "groups")

    moved = kernel_call(
        functools.partial(scores_kernel, block_len, dp_size),
        jax.ShapeDtypeStruct((3 * DEST_ROWS, QUERY_LANES), f32),
        [smem, smem] + [whole] * 12,
        whole,
        (live_tokens, move_plan, query_of_row.reshape(-1, 1), own_keep, own_got, near_keep, near_got,
         near_other, far_keep, far_got, far_other, last_keep, last_got, last_other),
    )
    moved = moved + swapped(moved, "tensor")
    kept, outer, inner = (moved[i * DEST_ROWS : (i + 1) * DEST_ROWS] for i in range(3))
    outer_pairs = [(d, (d + 1 if d % 2 else d - 1) % dp_size) for d in range(dp_size)]
    inner_pairs = [(d, d - 1 if d % 2 else d + 1) for d in range(dp_size)]
    total = kept + lax.ppermute(outer, "dp", outer_pairs) + lax.ppermute(inner, "dp", inner_pairs)
    return total[:slots_out, :QUERIES]


def shards(activations, out_grads, act_factor, grad_factor, query_of_row, live_tokens, move_plan):
    args = (activations, out_grads, act_factor, grad_factor, query_of_row, live_tokens, move_plan)
    dp_size = lax.axis_size("dp")
    tokens, act_width = activations.shape
    grad_width = out_grads.shape[1]
    rows = act_factor.shape[0]
    slots_in = live_tokens.shape[0]
    fits = (
        lax.axis_size("groups") == 2
        and lax.axis_size("tensor") == 2
        and dp_size % 2 == 0
        and 6 <= dp_size <= 16
        and act_width % (2 * LANES) == 0
        and grad_width % (2 * LANES) == 0
        and tokens == 2 * LANES
        and rows % SUBLANES == 0
        and slots_in % 4 == 0
        and slots_in <= 2 * DEST_ROWS
    )
    return ringed(*args) if fits else gathered(*args)


def solution(mesh):
    return jax.shard_map(
        shards,
        mesh=mesh,
        in_specs=(
            P(("groups", "dp"), "tensor"),
            P(("groups", "dp"), "tensor"),
            P("dp", "tensor"),
            P("dp", "tensor"),
            P(),
            P(("groups", "dp")),
            P(("groups", "dp"), None),
        ),
        out_specs=P(("groups", "dp"), None),
        check_vma=False,
    )
```

```python
import functools

import jax
import jax.numpy as jnp
from jax import lax
from jax.experimental import pallas as pl
from jax.experimental.pallas import tpu as pltpu
from jax.sharding import PartitionSpec as P

QUERIES = 20


def shifted(value, axis, steps):
    count = lax.axis_size(axis)
    pairs = [(source, (source + steps) % count) for source in range(count)]
    return lax.ppermute(value, axis, pairs)


def project_rows(rows, factor):
    return lax.dot_general(
        rows, factor, (((1,), (1,)), ((), ())), preferred_element_type=jnp.float32
    )


def swapped(value, axis):
    return lax.ppermute(value, axis, [(0, 1), (1, 0)])


def one_hot_queries(query_of_row):
    ids = jnp.arange(QUERIES, dtype=jnp.int32)[None, :]
    return (query_of_row[:, None] == ids).astype(jnp.float32)


def query_sums(rows, onehot):
    return jnp.dot(rows, onehot, precision=lax.Precision.HIGHEST, preferred_element_type=jnp.float32)


def gathered(activations, out_grads, act_factor, grad_factor, query_of_row, live_tokens, move_plan):
    slots_in = live_tokens.shape[0]
    block_len = activations.shape[0] // slots_in
    slots_out = slots_in // 2
    half_slots = slots_out // 2
    my_rank = lax.axis_index("dp")
    dp_size = lax.axis_size("dp")
    offsets = jnp.arange(block_len, dtype=jnp.int32)
    live_mask = (offsets[None, :] < live_tokens[:, None]).reshape(-1)
    grad_rows = jnp.where(live_mask[:, None], out_grads, jnp.zeros_like(out_grads))
    grad_all = lax.all_gather(grad_factor, "dp", axis=0, tiled=True)
    act_all = lax.all_gather(act_factor, "dp", axis=0, tiled=True)
    proj_grad = project_rows(grad_rows, grad_all)
    proj_act = project_rows(activations, act_all)
    full_grad, full_act = lax.psum((proj_grad, proj_act), "tensor")
    per_block = (full_grad * full_act).reshape(slots_in, block_len, -1).sum(axis=1)
    slot_scores = query_sums(per_block, one_hot_queries(query_of_row))
    keep, right, left = plan_weights(move_plan, my_rank, dp_size, slots_out, half_slots)
    lower = shifted(pick(right, slot_scores), "dp", 1)
    upper = shifted(pick(left, slot_scores), "dp", -1)
    return pick(keep, slot_scores) + jnp.concatenate([lower, upper], axis=0)


def plan_weights(move_plan, my_rank, dp_size, slots_out, half_slots):
    dest_rank = move_plan[:, 0]
    dest_slot = move_plan[:, 1]
    out_ids = jnp.arange(slots_out, dtype=jnp.int32)[:, None]
    hand_ids = jnp.arange(half_slots, dtype=jnp.int32)[:, None]
    keep = (dest_rank == my_rank)[None, :] & (dest_slot[None, :] == out_ids)
    right = (dest_rank == (my_rank + 1) % dp_size)[None, :] & (dest_slot[None, :] == hand_ids)
    left = (dest_rank == (my_rank + dp_size - 1) % dp_size)[None, :] & (
        dest_slot[None, :] == hand_ids + half_slots
    )
    return keep, right, left


def pick(hits, scores):
    return jnp.where(hits[:, :, None], scores[None, :, :], 0.0).sum(axis=1)


def ring_place(index, count):
    step = lax.div(index, 2)
    return jnp.where(lax.rem(index, 2) == 0, step, count - 1 - step)


def ring_index(place, count):
    place = lax.rem(place, count)
    return jnp.where(place < count // 2, 2 * place, 2 * (count - 1 - place) + 1)


LANES = 128
SUBLANES = 16
QUERY_LANES = 32
DEST_ROWS = 8


def after(value, *others):
    return lax.optimization_barrier((value, *others))[0]


def kernel_call(body, out_shape, in_specs, out_specs, operands, scratch=(), flops=0, limit=24):
    return pl.pallas_call(
        body,
        out_shape=out_shape,
        in_specs=in_specs,
        out_specs=out_specs,
        scratch_shapes=list(scratch),
        compiler_params=pltpu.CompilerParams(vmem_limit_bytes=limit * 1024 * 1024),
        cost_estimate=pl.CostEstimate(flops=flops, bytes_accessed=0, transcendentals=0),
    )(*operands)


def dot_rows(left, right):
    return lax.dot_general(
        left, right, (((1,), (1,)), ((), ())), preferred_element_type=jnp.float32
    )


def halves_kernel(acts, grads, act_factor, grad_factor, first, second, other, sems):
    act_half, grad_half = acts.shape[1] // 2, grads.shape[1] // 2
    cut = first.shape[1]
    group = lax.axis_index("groups")

    def columns(side, width, skip=0, size=None):
        return pl.ds(pl.multiple_of(side * width + skip, LANES), width if size is None else size)

    moves = [
        (act_factor.at[:, columns(group, act_half, 0, cut)], first),
        (act_factor.at[:, columns(group, act_half, cut, act_half - cut)], second.at[:, pl.ds(0, act_half - cut)]),
        (grad_factor.at[:, columns(group, grad_half)], second.at[:, pl.ds(act_half - cut, grad_half)]),
    ]
    size = acts.shape[0] // 4
    for part in range(4):
        some = pl.ds(part * size, size)
        moves += [
            (acts.at[some, columns(1 - group, act_half)], other.at[some, pl.ds(0, act_half)]),
            (grads.at[some, columns(1 - group, grad_half)], other.at[some, pl.ds(act_half, grad_half)]),
        ]
    copies = [pltpu.make_async_copy(src, dst, sems.at[i]) for i, (src, dst) in enumerate(moves)]
    for copy in copies:
        copy.start()
    for copy in copies:
        copy.wait()


def split_cores(act, grad, give, keep, sums, start):
    rows = act.shape[1]
    tokens = sums.shape[0]
    core = lax.axis_index("tensor")
    for i, value in enumerate((act, grad)):
        sums[:, :rows] = value
        for out, side in ((give, 1 - core), (keep, core)):
            some = sums[pl.ds(pl.multiple_of(side * (tokens // 2), LANES), tokens // 2), :]
            out[start + i * rows : start + (i + 1) * rows, :] = some.T[:rows]


def own_rows_kernel(acts, grads, act_factor, grad_factor, give, keep, own, sums):
    act_half, grad_half = acts.shape[1] // 2, grads.shape[1] // 2
    group = lax.axis_index("groups")
    act = dot_rows(acts[...], act_factor[...])
    grad = dot_rows(grads[...], grad_factor[...])
    split_cores(act, grad, give, keep, sums, 0)
    own[:, :act_half] = acts[:, pl.ds(pl.multiple_of(group * act_half, LANES), act_half)]
    own[:, act_half:] = grads[:, pl.ds(pl.multiple_of(group * grad_half, LANES), grad_half)]


def near_own_kernel(count, act_half, tokens, *refs):
    pieces, (factor, give, keep, sums, sems) = refs[:count], refs[count:]
    rows, cut = pieces[0].shape
    copies = []
    for i, piece in enumerate(pieces):
        columns = pl.ds(0, cut) if i % 2 == 0 else pl.ds(cut, factor.shape[1] - cut)
        copies.append(
            pltpu.make_async_copy(piece, factor.at[pl.ds(i // 2 * rows, rows), columns], sems.at[i])
        )
    for copy in copies:
        copy.start()
    for copy in copies:
        copy.wait()
    near_other_kernel(act_half, tokens, factor, give, keep, sums)


def near_other_kernel(act_half, tokens, factor, give, keep, sums):
    act = dot_rows(tokens[:, :act_half], factor[:, :act_half])
    grad = dot_rows(tokens[:, act_half:], factor[:, act_half:])
    split_cores(act, grad, give, keep, sums, 0)


def last_kernel(act_half, own, other, first, second, own_give, own_keep, give, keep, sums):
    rows, cut = first.shape
    rest = act_half - cut
    for i, tokens in enumerate((own, other)):
        act = dot_rows(tokens[:, :cut], first[...]) + dot_rows(tokens[:, cut:act_half], second[:, :rest])
        grad = dot_rows(tokens[:, act_half:], second[:, rest:])
        outs = (own_give, own_keep) if i == 0 else (give, keep)
        split_cores(act, grad, *outs, sums, 0)


def scores_kernel(block_len, dp_size, live_tokens, move_plan, query, *refs):
    exact = functools.partial(
        lax.dot_general, precision=lax.Precision.HIGHEST, preferred_element_type=jnp.float32
    )
    sets, out = refs[:-1], refs[-1]
    rows = sets[0].shape[0] // 2
    products = []
    for terms in (sets[:2], sets[2:5], sets[5:8], sets[8:]):
        size = terms[-1].shape[0]
        total = sum(term[:size, :] for term in terms)
        products.append(total[: size // 2] * total[size // 2 :])
    product = jnp.concatenate(products, axis=0)
    my_rank = lax.axis_index("dp")
    place = ring_place(my_rank, dp_size)
    distances = [0]
    for distance in range(1, dp_size // 2):
        distances += [-distance, distance]
    distances.append(dp_size // 2)
    ids = lax.broadcasted_iota(jnp.int32, (rows, QUERY_LANES), 1)
    onehots = []
    for distance in distances:
        start = ring_index(place + distance + dp_size, dp_size) * rows
        onehots.append((query[pl.ds(pl.multiple_of(start, 8), rows), :] == ids).astype(jnp.float32))
    sums = exact(jnp.concatenate(onehots, axis=0), product, (((0,), (0,)), ((), ())))
    tokens = sums.shape[1]
    slots = tokens // block_len
    token = lax.broadcasted_iota(jnp.int32, (3 * DEST_ROWS, tokens), 1)
    dest = lax.broadcasted_iota(jnp.int32, (3 * DEST_ROWS, tokens), 0)
    moves = jnp.zeros((3 * DEST_ROWS, tokens), jnp.float32)
    odd = lax.rem(my_rank, 2)
    partner = jnp.where(odd == 1, my_rank + 1, my_rank - 1 + dp_size)
    partner = lax.rem(partner, dp_size)
    for slot in range(slots):
        mine = lax.axis_index("tensor") * slots + slot
        rank = move_plan[mine, 0]
        side = jnp.where(rank == my_rank, 0, jnp.where(rank == partner, 1, 2))
        target = jnp.where(rank >= 0, side * DEST_ROWS + move_plan[mine, 1], -1)
        start = slot * block_len
        hit = (token >= start) & (token < start + live_tokens[mine]) & (dest == target)
        moves = moves + hit.astype(jnp.float32)
    out[...] = exact(moves, sums, (((1,), (1,)), ((), ())))


def ringed(activations, out_grads, act_factor, grad_factor, query_of_row, live_tokens, move_plan):
    dp_size = lax.axis_size("dp")
    slots_in = live_tokens.shape[0]
    tokens, act_width = activations.shape
    grad_width = out_grads.shape[1]
    rows = act_factor.shape[0]
    block_len = tokens // slots_in
    slots_out = slots_in // 2
    half = tokens // 2
    act_half, grad_half = act_width // 2, grad_width // 2
    width = act_half + grad_half
    cut = (width // 2) // LANES * LANES
    steps = dp_size // 2
    any_space = pl.BlockSpec(memory_space=pl.ANY)
    whole = pl.BlockSpec(memory_space=pltpu.VMEM)
    bf16, f32 = jnp.bfloat16, jnp.float32

    order = list(range(0, dp_size, 2)) + list(range(dp_size - 1, 0, -2))
    ahead = [(order[i], order[(i + 1) % dp_size]) for i in range(dp_size)]
    back = [(b, a) for a, b in ahead]
    smem = pl.BlockSpec(memory_space=pltpu.SMEM)

    first, second, other = kernel_call(
        halves_kernel,
        [
            jax.ShapeDtypeStruct((rows, cut), bf16),
            jax.ShapeDtypeStruct((rows, width - cut), bf16),
            jax.ShapeDtypeStruct((tokens, width), bf16),
        ],
        [any_space] * 4,
        [whole] * 3,
        (activations, out_grads, act_factor, grad_factor),
        scratch=[pltpu.SemaphoreType.DMA((11,))],
        limit=60,
    )
    other = swapped(other, "groups")

    def sent(pieces, pairs):
        return tuple(lax.ppermute(piece, "dp", pairs) for piece in pieces)

    start = (first, second)
    from_back, from_ahead = [start, sent(start, ahead)], [start, sent(start, back)]
    from_back.append(sent(from_back[1], ahead))
    from_ahead.append(sent(from_ahead[1], back))

    def work(factor_rows, features):
        return 2 * factor_rows * tokens * features

    halves = [jax.ShapeDtypeStruct((2 * rows, half), f32)] * 2
    sums = pltpu.VMEM((tokens, LANES), f32)
    own_give, own_keep, own = kernel_call(
        own_rows_kernel,
        halves + [jax.ShapeDtypeStruct((tokens, width), bf16)],
        [whole] * 4,
        [whole] * 3,
        lax.optimization_barrier(
            (activations, out_grads, act_factor, grad_factor, *from_back[1], *from_ahead[1])
        )[:4],
        scratch=[sums],
        flops=0 * work(rows, 2 * width),
    )
    own_got = swapped(own_give, "tensor")

    def tied(pieces, other):
        return [after(piece, other) for piece in pieces]

    def wide_sums(count):
        return pltpu.VMEM((tokens, -(-count // LANES) * LANES), f32)

    def against_own(pieces):
        count = rows * len(pieces) // 2
        factor, give, keep = kernel_call(
            functools.partial(near_own_kernel, len(pieces), act_half),
            [jax.ShapeDtypeStruct((count, width), bf16)] + [jax.ShapeDtypeStruct((2 * count, half), f32)] * 2,
            [whole] + [any_space] * len(pieces),
            [whole] * 3,
            (own, *pieces),
            scratch=[wide_sums(count), pltpu.SemaphoreType.DMA((len(pieces),))],
            flops=work(count, width),
        )
        return factor, give, keep, swapped(give, "tensor")

    def against_other(factor, other):
        count = factor.shape[0]
        give, keep = kernel_call(
            functools.partial(near_other_kernel, act_half),
            [jax.ShapeDtypeStruct((2 * count, half), f32)] * 2,
            [whole] * 2,
            [whole] * 2,
            (other, factor),
            scratch=[wide_sums(count)],
            flops=work(count, width),
        )
        total = keep + swapped(give, "tensor")
        return swapped(total, "groups"), total

    for distance in range(2, steps - 2):
        from_back.append(sent(from_back[distance], ahead))
        from_ahead.append(sent(from_ahead[distance], back))
    from_back.append(sent(tied(from_back[steps - 2], own_give), ahead))
    from_ahead.append(sent(tied(from_ahead[steps - 2], own_give), back))
    near_pieces = []
    for distance in range(1, steps - 1):
        near_pieces += [*from_back[distance], *from_ahead[distance]]
    near, near_give, near_keep, near_got = against_own(near_pieces)
    far_pieces = [*from_back[steps - 1], *from_ahead[steps - 1]]
    last_first, last_second = tied((from_back[-1][0], from_ahead[-1][1]), near_give)
    last = [lax.ppermute(last_first, "dp", ahead), lax.ppermute(last_second, "dp", back)]
    far, far_give, far_keep, far_got = against_own(far_pieces)
    other = after(other, far)
    far_other, far_total = against_other(far, other)
    near_other, near_total = against_other(near, other)

    last_give, last_keep, shared_give, shared_keep = kernel_call(
        functools.partial(last_kernel, act_half),
        [jax.ShapeDtypeStruct((2 * rows, half), f32)] * 4,
        [whole] * 4,
        [whole] * 4,
        (own, after(other, far_other), *last),
        scratch=[sums],
        flops=0,
    )
    last_got = swapped(last_give, "tensor")
    last_other = swapped(shared_keep + swapped(shared_give, "tensor"), "groups")

    moved = kernel_call(
        functools.partial(scores_kernel, block_len, dp_size),
        jax.ShapeDtypeStruct((3 * DEST_ROWS, QUERY_LANES), f32),
        [smem, smem] + [whole] * 12,
        whole,
        (live_tokens, move_plan, query_of_row.reshape(-1, 1), own_keep, own_got, near_keep, near_got,
         near_other, far_keep, far_got, far_other, last_keep, last_got, last_other),
    )
    moved = moved + swapped(moved, "tensor")
    kept, outer, inner = (moved[i * DEST_ROWS : (i + 1) * DEST_ROWS] for i in range(3))
    outer_pairs = [(d, (d + 1 if d % 2 else d - 1) % dp_size) for d in range(dp_size)]
    inner_pairs = [(d, d - 1 if d % 2 else d + 1) for d in range(dp_size)]
    total = kept + lax.ppermute(outer, "dp", outer_pairs) + lax.ppermute(inner, "dp", inner_pairs)
    return total[:slots_out, :QUERIES]


def shards(activations, out_grads, act_factor, grad_factor, query_of_row, live_tokens, move_plan):
    args = (activations, out_grads, act_factor, grad_factor, query_of_row, live_tokens, move_plan)
    dp_size = lax.axis_size("dp")
    tokens, act_width = activations.shape
    grad_width = out_grads.shape[1]
    rows = act_factor.shape[0]
    slots_in = live_tokens.shape[0]
    fits = (
        lax.axis_size("groups") == 2
        and lax.axis_size("tensor") == 2
        and dp_size % 2 == 0
        and 6 <= dp_size <= 16
        and act_width % (2 * LANES) == 0
        and grad_width % (2 * LANES) == 0
        and tokens == 2 * LANES
        and rows % SUBLANES == 0
        and slots_in % 4 == 0
        and slots_in <= 2 * DEST_ROWS
    )
    return ringed(*args) if fits else gathered(*args)


def solution(mesh):
    return jax.shard_map(
        shards,
        mesh=mesh,
        in_specs=(
            P(("groups", "dp"), "tensor"),
            P(("groups", "dp"), "tensor"),
            P("dp", "tensor"),
            P("dp", "tensor"),
            P(),
            P(("groups", "dp")),
            P(("groups", "dp"), None),
        ),
        out_specs=P(("groups", "dp"), None),
        check_vma=False,
    )
```

```python
import functools

import jax
import jax.numpy as jnp
from jax import lax
from jax.experimental import pallas as pl
from jax.experimental.pallas import tpu as pltpu
from jax.sharding import PartitionSpec as P

QUERIES = 20


def shifted(value, axis, steps):
    count = lax.axis_size(axis)
    pairs = [(source, (source + steps) % count) for source in range(count)]
    return lax.ppermute(value, axis, pairs)


def project_rows(rows, factor):
    return lax.dot_general(
        rows, factor, (((1,), (1,)), ((), ())), preferred_element_type=jnp.float32
    )


def swapped(value, axis):
    return lax.ppermute(value, axis, [(0, 1), (1, 0)])


def one_hot_queries(query_of_row):
    ids = jnp.arange(QUERIES, dtype=jnp.int32)[None, :]
    return (query_of_row[:, None] == ids).astype(jnp.float32)


def query_sums(rows, onehot):
    return jnp.dot(rows, onehot, precision=lax.Precision.HIGHEST, preferred_element_type=jnp.float32)


def gathered(activations, out_grads, act_factor, grad_factor, query_of_row, live_tokens, move_plan):
    slots_in = live_tokens.shape[0]
    block_len = activations.shape[0] // slots_in
    slots_out = slots_in // 2
    half_slots = slots_out // 2
    my_rank = lax.axis_index("dp")
    dp_size = lax.axis_size("dp")
    offsets = jnp.arange(block_len, dtype=jnp.int32)
    live_mask = (offsets[None, :] < live_tokens[:, None]).reshape(-1)
    grad_rows = jnp.where(live_mask[:, None], out_grads, jnp.zeros_like(out_grads))
    grad_all = lax.all_gather(grad_factor, "dp", axis=0, tiled=True)
    act_all = lax.all_gather(act_factor, "dp", axis=0, tiled=True)
    proj_grad = project_rows(grad_rows, grad_all)
    proj_act = project_rows(activations, act_all)
    full_grad, full_act = lax.psum((proj_grad, proj_act), "tensor")
    per_block = (full_grad * full_act).reshape(slots_in, block_len, -1).sum(axis=1)
    slot_scores = query_sums(per_block, one_hot_queries(query_of_row))
    keep, right, left = plan_weights(move_plan, my_rank, dp_size, slots_out, half_slots)
    lower = shifted(pick(right, slot_scores), "dp", 1)
    upper = shifted(pick(left, slot_scores), "dp", -1)
    return pick(keep, slot_scores) + jnp.concatenate([lower, upper], axis=0)


def plan_weights(move_plan, my_rank, dp_size, slots_out, half_slots):
    dest_rank = move_plan[:, 0]
    dest_slot = move_plan[:, 1]
    out_ids = jnp.arange(slots_out, dtype=jnp.int32)[:, None]
    hand_ids = jnp.arange(half_slots, dtype=jnp.int32)[:, None]
    keep = (dest_rank == my_rank)[None, :] & (dest_slot[None, :] == out_ids)
    right = (dest_rank == (my_rank + 1) % dp_size)[None, :] & (dest_slot[None, :] == hand_ids)
    left = (dest_rank == (my_rank + dp_size - 1) % dp_size)[None, :] & (
        dest_slot[None, :] == hand_ids + half_slots
    )
    return keep, right, left


def pick(hits, scores):
    return jnp.where(hits[:, :, None], scores[None, :, :], 0.0).sum(axis=1)


def ring_place(index, count):
    step = lax.div(index, 2)
    return jnp.where(lax.rem(index, 2) == 0, step, count - 1 - step)


def ring_index(place, count):
    place = lax.rem(place, count)
    return jnp.where(place < count // 2, 2 * place, 2 * (count - 1 - place) + 1)


LANES = 128
SUBLANES = 16
QUERY_LANES = 32
DEST_ROWS = 8


def after(value, *others):
    return lax.optimization_barrier((value, *others))[0]


def kernel_call(body, out_shape, in_specs, out_specs, operands, scratch=(), flops=0, limit=24):
    return pl.pallas_call(
        body,
        out_shape=out_shape,
        in_specs=in_specs,
        out_specs=out_specs,
        scratch_shapes=list(scratch),
        compiler_params=pltpu.CompilerParams(vmem_limit_bytes=limit * 1024 * 1024),
        cost_estimate=pl.CostEstimate(flops=flops, bytes_accessed=0, transcendentals=0),
    )(*operands)


def dot_rows(left, right):
    return lax.dot_general(
        left, right, (((1,), (1,)), ((), ())), preferred_element_type=jnp.float32
    )


def halves_kernel(acts, grads, act_factor, grad_factor, first, second, other, sems):
    act_half, grad_half = acts.shape[1] // 2, grads.shape[1] // 2
    cut = first.shape[1]
    group = lax.axis_index("groups")

    def columns(side, width, skip=0, size=None):
        return pl.ds(pl.multiple_of(side * width + skip, LANES), width if size is None else size)

    moves = [
        (act_factor.at[:, columns(group, act_half, 0, cut)], first),
        (act_factor.at[:, columns(group, act_half, cut, act_half - cut)], second.at[:, pl.ds(0, act_half - cut)]),
        (grad_factor.at[:, columns(group, grad_half)], second.at[:, pl.ds(act_half - cut, grad_half)]),
    ]
    size = acts.shape[0] // 4
    for part in range(4):
        some = pl.ds(part * size, size)
        moves += [
            (acts.at[some, columns(1 - group, act_half)], other.at[some, pl.ds(0, act_half)]),
            (grads.at[some, columns(1 - group, grad_half)], other.at[some, pl.ds(act_half, grad_half)]),
        ]
    copies = [pltpu.make_async_copy(src, dst, sems.at[i]) for i, (src, dst) in enumerate(moves)]
    for copy in copies:
        copy.start()
    for copy in copies:
        copy.wait()


def split_cores(act, grad, give, keep, sums, start):
    rows = act.shape[1]
    tokens = sums.shape[0]
    core = lax.axis_index("tensor")
    for i, value in enumerate((act, grad)):
        sums[:, :rows] = value
        for out, side in ((give, 1 - core), (keep, core)):
            some = sums[pl.ds(pl.multiple_of(side * (tokens // 2), LANES), tokens // 2), :]
            out[start + i * rows : start + (i + 1) * rows, :] = some.T[:rows]


def own_rows_kernel(acts, grads, act_factor, grad_factor, give, keep, own, sums):
    act_half, grad_half = acts.shape[1] // 2, grads.shape[1] // 2
    group = lax.axis_index("groups")
    act = dot_rows(acts[...], act_factor[...])
    grad = dot_rows(grads[...], grad_factor[...])
    split_cores(act, grad, give, keep, sums, 0)
    own[:, :act_half] = acts[:, pl.ds(pl.multiple_of(group * act_half, LANES), act_half)]
    own[:, act_half:] = grads[:, pl.ds(pl.multiple_of(group * grad_half, LANES), grad_half)]


def near_own_kernel(count, act_half, tokens, *refs):
    pieces, (factor, give, keep, sums, sems) = refs[:count], refs[count:]
    rows, cut = pieces[0].shape
    copies = []
    for i, piece in enumerate(pieces):
        columns = pl.ds(0, cut) if i % 2 == 0 else pl.ds(cut, factor.shape[1] - cut)
        copies.append(
            pltpu.make_async_copy(piece, factor.at[pl.ds(i // 2 * rows, rows), columns], sems.at[i])
        )
    for copy in copies:
        copy.start()
    for copy in copies:
        copy.wait()
    near_other_kernel(act_half, tokens, factor, give, keep, sums)


def near_other_kernel(act_half, tokens, factor, give, keep, sums):
    act = dot_rows(tokens[:, :act_half], factor[:, :act_half])
    grad = dot_rows(tokens[:, act_half:], factor[:, act_half:])
    split_cores(act, grad, give, keep, sums, 0)


def last_kernel(act_half, own, other, first, second, own_give, own_keep, give, keep, sums):
    rows, cut = first.shape
    rest = act_half - cut
    for i, tokens in enumerate((own, other)):
        act = dot_rows(tokens[:, :cut], first[...]) + dot_rows(tokens[:, cut:act_half], second[:, :rest])
        grad = dot_rows(tokens[:, act_half:], second[:, rest:])
        outs = (own_give, own_keep) if i == 0 else (give, keep)
        split_cores(act, grad, *outs, sums, 0)


def scores_kernel(block_len, dp_size, distances, counts, live_tokens, move_plan, query, *refs):
    exact = functools.partial(
        lax.dot_general, precision=lax.Precision.HIGHEST, preferred_element_type=jnp.float32
    )
    sets, before, out = refs[: sum(counts)], refs[sum(counts) : -1], refs[-1]
    products = []
    for count in counts:
        terms, sets = sets[:count], sets[count:]
        size = terms[-1].shape[0]
        total = sum(term[:size, :] for term in terms)
        products.append(total[: size // 2] * total[size // 2 :])
    rows = sum(value.shape[0] for value in products) // len(distances)
    product = jnp.concatenate(products, axis=0)
    my_rank = lax.axis_index("dp")
    place = ring_place(my_rank, dp_size)
    ids = lax.broadcasted_iota(jnp.int32, (rows, QUERY_LANES), 1)
    onehots = []
    for distance in distances:
        start = ring_index(place + distance + dp_size, dp_size) * rows
        onehots.append((query[pl.ds(pl.multiple_of(start, 8), rows), :] == ids).astype(jnp.float32))
    sums = exact(jnp.concatenate(onehots, axis=0), product, (((0,), (0,)), ((), ())))
    tokens = sums.shape[1]
    slots = tokens // block_len
    token = lax.broadcasted_iota(jnp.int32, (3 * DEST_ROWS, tokens), 1)
    dest = lax.broadcasted_iota(jnp.int32, (3 * DEST_ROWS, tokens), 0)
    moves = jnp.zeros((3 * DEST_ROWS, tokens), jnp.float32)
    odd = lax.rem(my_rank, 2)
    partner = jnp.where(odd == 1, my_rank + 1, my_rank - 1 + dp_size)
    partner = lax.rem(partner, dp_size)
    for slot in range(slots):
        mine = lax.axis_index("tensor") * slots + slot
        rank = move_plan[mine, 0]
        side = jnp.where(rank == my_rank, 0, jnp.where(rank == partner, 1, 2))
        target = jnp.where(rank >= 0, side * DEST_ROWS + move_plan[mine, 1], -1)
        start = slot * block_len
        hit = (token >= start) & (token < start + live_tokens[mine]) & (dest == target)
        moves = moves + hit.astype(jnp.float32)
    total = exact(moves, sums, (((1,), (1,)), ((), ())))
    for value in before:
        total = total + value[...]
    out[...] = total


def ringed(activations, out_grads, act_factor, grad_factor, query_of_row, live_tokens, move_plan):
    dp_size = lax.axis_size("dp")
    slots_in = live_tokens.shape[0]
    tokens, act_width = activations.shape
    grad_width = out_grads.shape[1]
    rows = act_factor.shape[0]
    block_len = tokens // slots_in
    slots_out = slots_in // 2
    half = tokens // 2
    act_half, grad_half = act_width // 2, grad_width // 2
    width = act_half + grad_half
    cut = (width // 2) // LANES * LANES
    steps = dp_size // 2
    any_space = pl.BlockSpec(memory_space=pl.ANY)
    whole = pl.BlockSpec(memory_space=pltpu.VMEM)
    bf16, f32 = jnp.bfloat16, jnp.float32

    order = list(range(0, dp_size, 2)) + list(range(dp_size - 1, 0, -2))
    ahead = [(order[i], order[(i + 1) % dp_size]) for i in range(dp_size)]
    back = [(b, a) for a, b in ahead]
    smem = pl.BlockSpec(memory_space=pltpu.SMEM)

    first, second, other = kernel_call(
        halves_kernel,
        [
            jax.ShapeDtypeStruct((rows, cut), bf16),
            jax.ShapeDtypeStruct((rows, width - cut), bf16),
            jax.ShapeDtypeStruct((tokens, width), bf16),
        ],
        [any_space] * 4,
        [whole] * 3,
        (activations, out_grads, act_factor, grad_factor),
        scratch=[pltpu.SemaphoreType.DMA((11,))],
        limit=60,
    )
    other = swapped(other, "groups")

    def sent(pieces, pairs):
        return tuple(lax.ppermute(piece, "dp", pairs) for piece in pieces)

    start = (first, second)
    from_back, from_ahead = [start, sent(start, ahead)], [start, sent(start, back)]
    from_back.append(sent(from_back[1], ahead))
    from_ahead.append(sent(from_ahead[1], back))

    def work(factor_rows, features):
        return 2 * factor_rows * tokens * features

    halves = [jax.ShapeDtypeStruct((2 * rows, half), f32)] * 2
    sums = pltpu.VMEM((tokens, LANES), f32)
    own_give, own_keep, own = kernel_call(
        own_rows_kernel,
        halves + [jax.ShapeDtypeStruct((tokens, width), bf16)],
        [whole] * 4,
        [whole] * 3,
        lax.optimization_barrier(
            (activations, out_grads, act_factor, grad_factor, *from_back[1], *from_ahead[1])
        )[:4],
        scratch=[sums],
        flops=0 * work(rows, 2 * width),
    )
    own_got = swapped(own_give, "tensor")

    def tied(pieces, other):
        return [after(piece, other) for piece in pieces]

    def wide_sums(count):
        return pltpu.VMEM((tokens, -(-count // LANES) * LANES), f32)

    def against_own(pieces):
        count = rows * len(pieces) // 2
        factor, give, keep = kernel_call(
            functools.partial(near_own_kernel, len(pieces), act_half),
            [jax.ShapeDtypeStruct((count, width), bf16)] + [jax.ShapeDtypeStruct((2 * count, half), f32)] * 2,
            [whole] + [any_space] * len(pieces),
            [whole] * 3,
            (own, *pieces),
            scratch=[wide_sums(count), pltpu.SemaphoreType.DMA((len(pieces),))],
            flops=work(count, width),
        )
        return factor, give, keep, swapped(give, "tensor")

    def against_other(factor, other):
        count = factor.shape[0]
        give, keep = kernel_call(
            functools.partial(near_other_kernel, act_half),
            [jax.ShapeDtypeStruct((2 * count, half), f32)] * 2,
            [whole] * 2,
            [whole] * 2,
            (other, factor),
            scratch=[wide_sums(count)],
            flops=work(count, width),
        )
        total = keep + swapped(give, "tensor")
        return swapped(total, "groups"), total

    for distance in range(2, steps - 2):
        from_back.append(sent(from_back[distance], ahead))
        from_ahead.append(sent(from_ahead[distance], back))
    from_back.append(sent(tied(from_back[steps - 2], own_give), ahead))
    from_ahead.append(sent(tied(from_ahead[steps - 2], own_give), back))
    near_pieces = []
    for distance in range(1, steps - 1):
        near_pieces += [*from_back[distance], *from_ahead[distance]]
    near, near_give, near_keep, near_got = against_own(near_pieces)
    far_pieces = [*from_back[steps - 1], *from_ahead[steps - 1]]
    last_first, last_second = tied((from_back[-1][0], from_ahead[-1][1]), near_give)
    last = [lax.ppermute(last_first, "dp", ahead), lax.ppermute(last_second, "dp", back)]
    far, far_give, far_keep, far_got = against_own(far_pieces)
    other = after(other, far)
    far_other, far_total = against_other(far, other)
    near_other, near_total = against_other(near, other)

    last_give, last_keep, shared_give, shared_keep = kernel_call(
        functools.partial(last_kernel, act_half),
        [jax.ShapeDtypeStruct((2 * rows, half), f32)] * 4,
        [whole] * 4,
        [whole] * 4,
        (own, after(other, far_other), *last),
        scratch=[sums],
        flops=0,
    )
    last_got = swapped(last_give, "tensor")
    last_other = swapped(shared_keep + swapped(shared_give, "tensor"), "groups")

    distances = [0]
    for distance in range(1, steps):
        distances += [-distance, distance]

    def scores(distances, counts, terms, flops=0):
        return kernel_call(
            functools.partial(scores_kernel, block_len, dp_size, distances, counts),
            jax.ShapeDtypeStruct((3 * DEST_ROWS, QUERY_LANES), f32),
            [smem, smem] + [whole] * (1 + len(terms)),
            whole,
            (live_tokens, move_plan, query_of_row.reshape(-1, 1), *terms),
            flops=flops,
        )

    moved = scores(
        distances,
        (2, 3, 3),
        (own_keep, own_got, near_keep, near_got, near_other, far_keep, far_got, far_other),
        flops=work(rows, width),
    )
    moved = scores([steps], (3,), (last_keep, last_got, last_other, moved))
    moved = moved + swapped(moved, "tensor")
    kept, outer, inner = (moved[i * DEST_ROWS : (i + 1) * DEST_ROWS] for i in range(3))
    outer_pairs = [(d, (d + 1 if d % 2 else d - 1) % dp_size) for d in range(dp_size)]
    inner_pairs = [(d, d - 1 if d % 2 else d + 1) for d in range(dp_size)]
    total = kept + lax.ppermute(outer, "dp", outer_pairs) + lax.ppermute(inner, "dp", inner_pairs)
    return total[:slots_out, :QUERIES]


def shards(activations, out_grads, act_factor, grad_factor, query_of_row, live_tokens, move_plan):
    args = (activations, out_grads, act_factor, grad_factor, query_of_row, live_tokens, move_plan)
    dp_size = lax.axis_size("dp")
    tokens, act_width = activations.shape
    grad_width = out_grads.shape[1]
    rows = act_factor.shape[0]
    slots_in = live_tokens.shape[0]
    fits = (
        lax.axis_size("groups") == 2
        and lax.axis_size("tensor") == 2
        and dp_size % 2 == 0
        and 6 <= dp_size <= 16
        and act_width % (2 * LANES) == 0
        and grad_width % (2 * LANES) == 0
        and tokens == 2 * LANES
        and rows % SUBLANES == 0
        and slots_in % 4 == 0
        and slots_in <= 2 * DEST_ROWS
    )
    return ringed(*args) if fits else gathered(*args)


def solution(mesh):
    return jax.shard_map(
        shards,
        mesh=mesh,
        in_specs=(
            P(("groups", "dp"), "tensor"),
            P(("groups", "dp"), "tensor"),
            P("dp", "tensor"),
            P("dp", "tensor"),
            P(),
            P(("groups", "dp")),
            P(("groups", "dp"), None),
        ),
        out_specs=P(("groups", "dp"), None),
        check_vma=False,
    )
```

```python
import functools

import jax
import jax.numpy as jnp
from jax import lax
from jax.experimental import pallas as pl
from jax.experimental.pallas import tpu as pltpu
from jax.sharding import PartitionSpec as P

QUERIES = 20


def shifted(value, axis, steps):
    count = lax.axis_size(axis)
    pairs = [(source, (source + steps) % count) for source in range(count)]
    return lax.ppermute(value, axis, pairs)


def project_rows(rows, factor):
    return lax.dot_general(
        rows, factor, (((1,), (1,)), ((), ())), preferred_element_type=jnp.float32
    )


def swapped(value, axis):
    return lax.ppermute(value, axis, [(0, 1), (1, 0)])


def one_hot_queries(query_of_row):
    ids = jnp.arange(QUERIES, dtype=jnp.int32)[None, :]
    return (query_of_row[:, None] == ids).astype(jnp.float32)


def query_sums(rows, onehot):
    return jnp.dot(rows, onehot, precision=lax.Precision.HIGHEST, preferred_element_type=jnp.float32)


def gathered(activations, out_grads, act_factor, grad_factor, query_of_row, live_tokens, move_plan):
    slots_in = live_tokens.shape[0]
    block_len = activations.shape[0] // slots_in
    slots_out = slots_in // 2
    half_slots = slots_out // 2
    my_rank = lax.axis_index("dp")
    dp_size = lax.axis_size("dp")
    offsets = jnp.arange(block_len, dtype=jnp.int32)
    live_mask = (offsets[None, :] < live_tokens[:, None]).reshape(-1)
    grad_rows = jnp.where(live_mask[:, None], out_grads, jnp.zeros_like(out_grads))
    grad_all = lax.all_gather(grad_factor, "dp", axis=0, tiled=True)
    act_all = lax.all_gather(act_factor, "dp", axis=0, tiled=True)
    proj_grad = project_rows(grad_rows, grad_all)
    proj_act = project_rows(activations, act_all)
    full_grad, full_act = lax.psum((proj_grad, proj_act), "tensor")
    per_block = (full_grad * full_act).reshape(slots_in, block_len, -1).sum(axis=1)
    slot_scores = query_sums(per_block, one_hot_queries(query_of_row))
    keep, right, left = plan_weights(move_plan, my_rank, dp_size, slots_out, half_slots)
    lower = shifted(pick(right, slot_scores), "dp", 1)
    upper = shifted(pick(left, slot_scores), "dp", -1)
    return pick(keep, slot_scores) + jnp.concatenate([lower, upper], axis=0)


def plan_weights(move_plan, my_rank, dp_size, slots_out, half_slots):
    dest_rank = move_plan[:, 0]
    dest_slot = move_plan[:, 1]
    out_ids = jnp.arange(slots_out, dtype=jnp.int32)[:, None]
    hand_ids = jnp.arange(half_slots, dtype=jnp.int32)[:, None]
    keep = (dest_rank == my_rank)[None, :] & (dest_slot[None, :] == out_ids)
    right = (dest_rank == (my_rank + 1) % dp_size)[None, :] & (dest_slot[None, :] == hand_ids)
    left = (dest_rank == (my_rank + dp_size - 1) % dp_size)[None, :] & (
        dest_slot[None, :] == hand_ids + half_slots
    )
    return keep, right, left


def pick(hits, scores):
    return jnp.where(hits[:, :, None], scores[None, :, :], 0.0).sum(axis=1)


def ring_place(index, count):
    step = lax.div(index, 2)
    return jnp.where(lax.rem(index, 2) == 0, step, count - 1 - step)


def ring_index(place, count):
    place = lax.rem(place, count)
    return jnp.where(place < count // 2, 2 * place, 2 * (count - 1 - place) + 1)


LANES = 128
SUBLANES = 16
QUERY_LANES = 32
DEST_ROWS = 8


def after(value, *others):
    return lax.optimization_barrier((value, *others))[0]


def kernel_call(body, out_shape, in_specs, out_specs, operands, scratch=(), flops=0, limit=24):
    return pl.pallas_call(
        body,
        out_shape=out_shape,
        in_specs=in_specs,
        out_specs=out_specs,
        scratch_shapes=list(scratch),
        compiler_params=pltpu.CompilerParams(vmem_limit_bytes=limit * 1024 * 1024),
        cost_estimate=pl.CostEstimate(flops=flops, bytes_accessed=0, transcendentals=0),
    )(*operands)


def dot_rows(left, right):
    return lax.dot_general(
        left, right, (((1,), (1,)), ((), ())), preferred_element_type=jnp.float32
    )


def halves_kernel(acts, grads, act_factor, grad_factor, first, second, other, sems):
    act_half, grad_half = acts.shape[1] // 2, grads.shape[1] // 2
    cut = first.shape[1]
    group = lax.axis_index("groups")

    def columns(side, width, skip=0, size=None):
        return pl.ds(pl.multiple_of(side * width + skip, LANES), width if size is None else size)

    moves = [
        (act_factor.at[:, columns(group, act_half, 0, cut)], first),
        (act_factor.at[:, columns(group, act_half, cut, act_half - cut)], second.at[:, pl.ds(0, act_half - cut)]),
        (grad_factor.at[:, columns(group, grad_half)], second.at[:, pl.ds(act_half - cut, grad_half)]),
    ]
    size = acts.shape[0] // 4
    for part in range(4):
        some = pl.ds(part * size, size)
        moves += [
            (acts.at[some, columns(1 - group, act_half)], other.at[some, pl.ds(0, act_half)]),
            (grads.at[some, columns(1 - group, grad_half)], other.at[some, pl.ds(act_half, grad_half)]),
        ]
    copies = [pltpu.make_async_copy(src, dst, sems.at[i]) for i, (src, dst) in enumerate(moves)]
    for copy in copies:
        copy.start()
    for copy in copies:
        copy.wait()


def split_cores(act, grad, give, keep, sums, start):
    rows = act.shape[1]
    tokens = sums.shape[0]
    core = lax.axis_index("tensor")
    for i, value in enumerate((act, grad)):
        sums[:, :rows] = value
        for out, side in ((give, 1 - core), (keep, core)):
            some = sums[pl.ds(pl.multiple_of(side * (tokens // 2), LANES), tokens // 2), :]
            out[start + i * rows : start + (i + 1) * rows, :] = some.T[:rows]


def own_rows_kernel(acts, grads, act_factor, grad_factor, give, keep, own, sums):
    act_half, grad_half = acts.shape[1] // 2, grads.shape[1] // 2
    group = lax.axis_index("groups")
    act = dot_rows(acts[...], act_factor[...])
    grad = dot_rows(grads[...], grad_factor[...])
    split_cores(act, grad, give, keep, sums, 0)
    own[:, :act_half] = acts[:, pl.ds(pl.multiple_of(group * act_half, LANES), act_half)]
    own[:, act_half:] = grads[:, pl.ds(pl.multiple_of(group * grad_half, LANES), grad_half)]


def near_own_kernel(count, act_half, tokens, *refs):
    pieces, (factor, give, keep, sums, sems) = refs[:count], refs[count:]
    rows, cut = pieces[0].shape
    copies = []
    for i, piece in enumerate(pieces):
        columns = pl.ds(0, cut) if i % 2 == 0 else pl.ds(cut, factor.shape[1] - cut)
        copies.append(
            pltpu.make_async_copy(piece, factor.at[pl.ds(i // 2 * rows, rows), columns], sems.at[i])
        )
    for copy in copies:
        copy.start()
    for copy in copies:
        copy.wait()
    near_other_kernel(act_half, tokens, factor, give, keep, sums)


def near_other_kernel(act_half, tokens, factor, give, keep, sums):
    act = dot_rows(tokens[:, :act_half], factor[:, :act_half])
    grad = dot_rows(tokens[:, act_half:], factor[:, act_half:])
    split_cores(act, grad, give, keep, sums, 0)


def last_kernel(act_half, own, other, first, second, own_give, own_keep, give, keep, sums):
    rows, cut = first.shape
    rest = act_half - cut
    for i, tokens in enumerate((own, other)):
        act = dot_rows(tokens[:, :cut], first[...]) + dot_rows(tokens[:, cut:act_half], second[:, :rest])
        grad = dot_rows(tokens[:, act_half:], second[:, rest:])
        outs = (own_give, own_keep) if i == 0 else (give, keep)
        split_cores(act, grad, *outs, sums, 0)


def scores_kernel(block_len, dp_size, live_tokens, move_plan, query, *refs):
    exact = functools.partial(
        lax.dot_general, precision=lax.Precision.HIGHEST, preferred_element_type=jnp.float32
    )
    sets, out = refs[:-1], refs[-1]
    rows = sets[0].shape[0] // 2
    products = []
    for terms in (sets[:2], sets[2:5], sets[5:8], sets[8:]):
        size = terms[-1].shape[0]
        total = sum(term[:size, :] for term in terms)
        products.append(total[: size // 2] * total[size // 2 :])
    product = jnp.concatenate(products, axis=0)
    my_rank = lax.axis_index("dp")
    place = ring_place(my_rank, dp_size)
    distances = [0]
    for distance in range(1, dp_size // 2):
        distances += [-distance, distance]
    distances.append(dp_size // 2)
    ids = lax.broadcasted_iota(jnp.int32, (rows, QUERY_LANES), 1)
    onehots = []
    for distance in distances:
        start = ring_index(place + distance + dp_size, dp_size) * rows
        onehots.append((query[pl.ds(pl.multiple_of(start, 8), rows), :] == ids).astype(jnp.float32))
    sums = exact(jnp.concatenate(onehots, axis=0), product, (((0,), (0,)), ((), ())))
    tokens = sums.shape[1]
    slots = tokens // block_len
    token = lax.broadcasted_iota(jnp.int32, (3 * DEST_ROWS, tokens), 1)
    dest = lax.broadcasted_iota(jnp.int32, (3 * DEST_ROWS, tokens), 0)
    moves = jnp.zeros((3 * DEST_ROWS, tokens), jnp.float32)
    odd = lax.rem(my_rank, 2)
    partner = jnp.where(odd == 1, my_rank + 1, my_rank - 1 + dp_size)
    partner = lax.rem(partner, dp_size)
    for slot in range(slots):
        mine = lax.axis_index("tensor") * slots + slot
        rank = move_plan[mine, 0]
        side = jnp.where(rank == my_rank, 0, jnp.where(rank == partner, 1, 2))
        target = jnp.where(rank >= 0, side * DEST_ROWS + move_plan[mine, 1], -1)
        start = slot * block_len
        hit = (token >= start) & (token < start + live_tokens[mine]) & (dest == target)
        moves = moves + hit.astype(jnp.float32)
    out[...] = exact(moves, sums, (((1,), (1,)), ((), ())))


def ringed(activations, out_grads, act_factor, grad_factor, query_of_row, live_tokens, move_plan):
    dp_size = lax.axis_size("dp")
    slots_in = live_tokens.shape[0]
    tokens, act_width = activations.shape
    grad_width = out_grads.shape[1]
    rows = act_factor.shape[0]
    block_len = tokens // slots_in
    slots_out = slots_in // 2
    half = tokens // 2
    act_half, grad_half = act_width // 2, grad_width // 2
    width = act_half + grad_half
    cut = (width // 2) // LANES * LANES
    steps = dp_size // 2
    any_space = pl.BlockSpec(memory_space=pl.ANY)
    whole = pl.BlockSpec(memory_space=pltpu.VMEM)
    bf16, f32 = jnp.bfloat16, jnp.float32

    order = list(range(0, dp_size, 2)) + list(range(dp_size - 1, 0, -2))
    ahead = [(order[i], order[(i + 1) % dp_size]) for i in range(dp_size)]
    back = [(b, a) for a, b in ahead]
    smem = pl.BlockSpec(memory_space=pltpu.SMEM)

    first, second, other = kernel_call(
        halves_kernel,
        [
            jax.ShapeDtypeStruct((rows, cut), bf16),
            jax.ShapeDtypeStruct((rows, width - cut), bf16),
            jax.ShapeDtypeStruct((tokens, width), bf16),
        ],
        [any_space] * 4,
        [whole] * 3,
        (activations, out_grads, act_factor, grad_factor),
        scratch=[pltpu.SemaphoreType.DMA((11,))],
        limit=60,
    )
    other = swapped(other, "groups")

    def sent(pieces, pairs):
        return tuple(lax.ppermute(piece, "dp", pairs) for piece in pieces)

    start = (first, second)
    from_back, from_ahead = [start, sent(start, ahead)], [start, sent(start, back)]
    from_back.append(sent(from_back[1], ahead))
    from_ahead.append(sent(from_ahead[1], back))

    def work(factor_rows, features):
        return 2 * factor_rows * tokens * features

    halves = [jax.ShapeDtypeStruct((2 * rows, half), f32)] * 2
    sums = pltpu.VMEM((tokens, LANES), f32)
    own_give, own_keep, own = kernel_call(
        own_rows_kernel,
        halves + [jax.ShapeDtypeStruct((tokens, width), bf16)],
        [whole] * 4,
        [whole] * 3,
        lax.optimization_barrier(
            (activations, out_grads, act_factor, grad_factor, *from_back[1], *from_ahead[1])
        )[:4],
        scratch=[sums],
        flops=0,
    )
    own_got = swapped(own_give, "tensor")

    def tied(pieces, other):
        return [after(piece, other) for piece in pieces]

    def wide_sums(count):
        return pltpu.VMEM((tokens, -(-count // LANES) * LANES), f32)

    def against_own(pieces):
        count = rows * len(pieces) // 2
        factor, give, keep = kernel_call(
            functools.partial(near_own_kernel, len(pieces), act_half),
            [jax.ShapeDtypeStruct((count, width), bf16)] + [jax.ShapeDtypeStruct((2 * count, half), f32)] * 2,
            [whole] + [any_space] * len(pieces),
            [whole] * 3,
            (own, *pieces),
            scratch=[wide_sums(count), pltpu.SemaphoreType.DMA((len(pieces),))],
            flops=work(count, width),
        )
        return factor, give, keep, swapped(give, "tensor")

    def against_other(factor, other):
        count = factor.shape[0]
        give, keep = kernel_call(
            functools.partial(near_other_kernel, act_half),
            [jax.ShapeDtypeStruct((2 * count, half), f32)] * 2,
            [whole] * 2,
            [whole] * 2,
            (other, factor),
            scratch=[wide_sums(count)],
            flops=work(count, width),
        )
        total = keep + swapped(give, "tensor")
        return swapped(total, "groups"), total

    for distance in range(2, steps - 2):
        from_back.append(sent(from_back[distance], ahead))
        from_ahead.append(sent(from_ahead[distance], back))
    from_back.append(sent(tied(from_back[steps - 2], own_give), ahead))
    from_ahead.append(sent(tied(from_ahead[steps - 2], own_give), back))
    near_pieces = []
    for distance in range(1, steps - 1):
        near_pieces += [*from_back[distance], *from_ahead[distance]]
    near, near_give, near_keep, near_got = against_own(near_pieces)
    far_pieces = [*from_back[steps - 1], *from_ahead[steps - 1]]
    last_first, last_second = tied((from_back[-1][0], from_ahead[-1][1]), near_give)
    last = [lax.ppermute(last_first, "dp", ahead), lax.ppermute(last_second, "dp", back)]
    far, far_give, far_keep, far_got = against_own(far_pieces)
    other = after(other, from_back[-1][0], from_ahead[-1][1])
    far_other, far_total = against_other(far, other)
    near_other, near_total = against_other(near, other)

    last_give, last_keep, shared_give, shared_keep = kernel_call(
        functools.partial(last_kernel, act_half),
        [jax.ShapeDtypeStruct((2 * rows, half), f32)] * 4,
        [whole] * 4,
        [whole] * 4,
        (own, after(other, far_other), *last),
        scratch=[sums],
        flops=64 * work(rows, width),
    )
    last_got = swapped(last_give, "tensor")
    last_other = swapped(shared_keep + swapped(shared_give, "tensor"), "groups")

    moved = kernel_call(
        functools.partial(scores_kernel, block_len, dp_size),
        jax.ShapeDtypeStruct((3 * DEST_ROWS, QUERY_LANES), f32),
        [smem, smem] + [whole] * 12,
        whole,
        (live_tokens, move_plan, query_of_row.reshape(-1, 1), own_keep, own_got, near_keep, near_got,
         near_other, far_keep, far_got, far_other, last_keep, last_got, last_other),
    )
    moved = moved + swapped(moved, "tensor")
    kept, outer, inner = (moved[i * DEST_ROWS : (i + 1) * DEST_ROWS] for i in range(3))
    outer_pairs = [(d, (d + 1 if d % 2 else d - 1) % dp_size) for d in range(dp_size)]
    inner_pairs = [(d, d - 1 if d % 2 else d + 1) for d in range(dp_size)]
    total = kept + lax.ppermute(outer, "dp", outer_pairs) + lax.ppermute(inner, "dp", inner_pairs)
    return total[:slots_out, :QUERIES]


def shards(activations, out_grads, act_factor, grad_factor, query_of_row, live_tokens, move_plan):
    args = (activations, out_grads, act_factor, grad_factor, query_of_row, live_tokens, move_plan)
    dp_size = lax.axis_size("dp")
    tokens, act_width = activations.shape
    grad_width = out_grads.shape[1]
    rows = act_factor.shape[0]
    slots_in = live_tokens.shape[0]
    fits = (
        lax.axis_size("groups") == 2
        and lax.axis_size("tensor") == 2
        and dp_size % 2 == 0
        and 6 <= dp_size <= 16
        and act_width % (2 * LANES) == 0
        and grad_width % (2 * LANES) == 0
        and tokens == 2 * LANES
        and rows % SUBLANES == 0
        and slots_in % 4 == 0
        and slots_in <= 2 * DEST_ROWS
    )
    return ringed(*args) if fits else gathered(*args)


def solution(mesh):
    return jax.shard_map(
        shards,
        mesh=mesh,
        in_specs=(
            P(("groups", "dp"), "tensor"),
            P(("groups", "dp"), "tensor"),
            P("dp", "tensor"),
            P("dp", "tensor"),
            P(),
            P(("groups", "dp")),
            P(("groups", "dp"), None),
        ),
        out_specs=P(("groups", "dp"), None),
        check_vma=False,
    )
```
